512 devices in a mesh: blk: 8 (over y, core), dp: 32 (over x_lo, z), mp: 2 (over x_hi).
Axes of the slice: x: 4 (x_hi: 2, x_lo: 2; x = x_hi * 2 + x_lo), y: 4, z: 16, core: 2. Of those that a mesh axis runs over, the one named last changes fastest.
Arguments:
- residual_tokens: bfloat16 [32, 8, 640, 1152], P('dp', 'blk'), may hold values from -20 to 20
- patch_tallies: int32 [32, 8], P('dp', 'blk'), may hold values from 106 to 640, as said below
- picture_assignment: int32 [32, 8, 640], P('dp', 'blk'), may hold values from 0 to 8, as said below
- normalizer_multiplier: float32 [1152], replicated, may hold values from 0.1 to 1.9
- expanding_matrix: bfloat16 [1152, 4304], P('dp', 'mp'), may hold values from -0.1875 to 0.1875
- contracting_matrix: bfloat16 [4304, 1152], P('mp', 'dp'), may hold values from -0.09375 to 0.09375
- sentence_vectors: bfloat16 [32, 64, 1152], P('dp', ('blk', 'mp')), may hold values from -20 to 20
- described_picture_number: int32 [32, 64], P('dp', ('blk', 'mp')), may hold values from 0 to 63
- similarity_multiplier: float32 [1], replicated, may hold values from 8 to 16
- additive_shift_term: float32 [1], replicated, may hold values from -4 to -1
Outputs:
- image_features: float32 [32, 64, 1152], P('dp', ('blk', 'mp'))
- image_grads: float32 [32, 64, 1152], P('dp', ('blk', 'mp'))
- text_grads: float32 [32, 64, 1152], P('dp', ('blk', 'mp'))
The draws below stay inside these ranges and needn't reach their ends.
Inputs may be any that keep to these rules, and one draw needn't show every extreme that they name: `patch_tallies`: at least one pack is full. `picture_assignment`: along a pack the ids never fall; its first patch_tallies[g, b] rows hold 7 or 8 images numbered from 0, each covering one or more of those rows; the other rows hold 8.
All inputs are finite; a program needn't handle non-finite values.
Results may differ from the reference program's by a relative error of at most 0.015.
Values may be sent and summed in bfloat16 or wider, within the bound.
A program may use at most 64 MiB of HBM per device.

```python
import jax
import jax.numpy as jnp
from jax import lax

D = 1152
FF = 4304
ROWS = 640
GROUPS = 32
PACKS_GROUP = 8
IMG_PACK = 8
GROUP = 64


def pack_layout(key):
    keys = jax.random.split(jax.random.fold_in(key, 101), 4)
    packs = GROUPS * PACKS_GROUP
    factors = jax.random.randint(keys[0], (3, packs), 0, 64)
    product = factors[0] * factors[1] * factors[2]
    lowest = ROWS // 6
    patch_tallies = lowest + product * (ROWS - lowest) // 250047
    fullest = jax.random.randint(keys[1], (), 0, packs)
    patch_tallies = jnp.where(jnp.arange(packs) == fullest, ROWS, patch_tallies)
    images = IMG_PACK - (jax.random.randint(keys[2], (packs,), 0, 4) == 0).astype(jnp.int32)
    orders = jnp.arange(1, IMG_PACK)
    reach = jnp.maximum(patch_tallies // (2 * images), 1)
    jitter = jax.random.randint(keys[3], (packs, IMG_PACK - 1), 0, 65536) % reach[:, None]
    starts = jnp.where(orders[None, :] < images[:, None], patch_tallies[:, None] * orders[None, :] // images[:, None] + jitter, ROWS + 1)
    positions = jnp.arange(ROWS)
    inside = jnp.sum((positions[None, :, None] >= starts[:, None, :]).astype(jnp.int32), axis=2)
    slot_ids = jnp.where(positions[None, :] < patch_tallies[:, None], inside, IMG_PACK)
    return (patch_tallies.reshape(GROUPS, PACKS_GROUP).astype(jnp.int32), slot_ids.reshape(GROUPS, PACKS_GROUP, ROWS).astype(jnp.int32))


def spread_scales(row_key, column_key, shape):
    row_shape = shape[:-1] + (1,)
    column_shape = (1,) * (len(shape) - 1) + (shape[-1],)
    row_scale = jnp.exp(jax.random.uniform(row_key, row_shape, minval=0.0, maxval=2.302585))
    column_scale = jnp.exp(jax.random.uniform(column_key, column_shape, minval=0.0, maxval=2.302585))
    return row_scale * column_scale


def draw_patch_tallies(key, part):
    layout = pack_layout(key)
    return layout[0]


def draw_picture_assignment(key, part):
    layout = pack_layout(key)
    return layout[1]


def draw_residual_tokens(key, part):
    key = jax.random.fold_in(key, 7)
    keys = jax.random.split(key, 3)
    shape = (GROUPS, PACKS_GROUP, ROWS, D)
    scales = spread_scales(keys[1], keys[2], shape)
    values = jnp.clip(jax.random.normal(keys[0], shape), -4.0, 4.0) * scales * 0.05
    return values.astype(jnp.bfloat16)


def draw_sentence_vectors(key, part):
    key = jax.random.fold_in(key, 9)
    keys = jax.random.split(key, 3)
    shape = (GROUPS, GROUP, D)
    scales = spread_scales(keys[1], keys[2], shape)
    values = jnp.clip(jax.random.normal(keys[0], shape), -4.0, 4.0) * scales * 0.05
    return values.astype(jnp.bfloat16)


def with_ends(entries, key, least, largest):
    place = [jax.random.randint(jax.random.fold_in(key, axis), (), 0, length) for axis, length in enumerate(entries.shape)]
    main_axis = entries.shape.index(max(entries.shape))
    next_to = place[:main_axis] + [(place[main_axis] + 1) % entries.shape[main_axis]] + place[main_axis + 1:]
    return entries.at[tuple(place)].set(least).at[tuple(next_to)].set(largest)


def steps_of(key, shape, cuts, least, high):
    def one(axis_at, shards_of):
        draws = jax.random.uniform(jax.random.fold_in(jax.random.fold_in(key, 6), axis_at), (shards_of,), jnp.float32, least / len(cuts), high / len(cuts))
        return jnp.repeat(jnp.exp(draws), shape[axis_at] // shards_of).reshape((-1,) + (1,) * (len(shape) - axis_at - 1))

    gain = one(*cuts[0])
    for cut in cuts[1:]:
        gain = gain * one(*cut)
    return gain


def scatter_about(own_key, dims, scale, limit, cuts=(), kind=jnp.bfloat16):
    gain = steps_of(own_key, dims, cuts, -0.22, 0.18) if cuts else 1.0
    drawn = jax.random.normal(own_key, dims, jnp.float32) * scale * gain
    return jnp.minimum(jnp.maximum(drawn, -limit), limit).astype(kind)


def setup_inputs(seed: int = 0) -> dict:
    seeds = jax.random.split(jax.random.key(seed), 11)
    residual_tokens = draw_residual_tokens(jax.random.fold_in(seeds[10], 71), 0)
    patch_tallies = draw_patch_tallies(jax.random.fold_in(seeds[10], 71), 0)
    picture_assignment = draw_picture_assignment(jax.random.fold_in(seeds[10], 71), 0)
    normalizer_multiplier = jnp.clip(1.0 + 0.18 * jax.random.normal(seeds[3], (D,), jnp.float32), 0.1, 1.9)
    expanding_matrix = scatter_about(seeds[4], (D, FF), D ** -0.5, 0.1875, ((0, 32), (1, 2)))
    contracting_matrix = scatter_about(seeds[5], (FF, D), FF ** -0.5, 0.09375, ((0, 2), (1, 32)))
    sentence_vectors = draw_sentence_vectors(jax.random.fold_in(seeds[10], 71), 0)
    described_picture_number = with_ends(jax.random.randint(seeds[7], (GROUPS, GROUP), 0, GROUP), jax.random.fold_in(seeds[7], 1), 0, GROUP - 1).astype(jnp.int32)
    similarity_multiplier = jnp.clip(jax.random.uniform(seeds[8], (1,), jnp.float32, 8.0, 16.0), 8.0, 16.0)
    additive_shift_term = jnp.clip(jax.random.uniform(seeds[9], (1,), jnp.float32, -4.0, -1.0), -4.0, -1.0)
    return {"residual_tokens": residual_tokens, "patch_tallies": patch_tallies, "picture_assignment": picture_assignment, "normalizer_multiplier": normalizer_multiplier, "expanding_matrix": expanding_matrix, "contracting_matrix": contracting_matrix, "sentence_vectors": sentence_vectors, "described_picture_number": described_picture_number, "similarity_multiplier": similarity_multiplier, "additive_shift_term": additive_shift_term}


highest = lax.Precision.HIGHEST

def pack_features(pack_rows, count, slot_ids, normalizer_multiplier, expanding_matrix, contracting_matrix):
    values = pack_rows.astype(jnp.float32)
    center = values - lax.optimization_barrier(jnp.mean(values, axis=1, keepdims=True))
    spread = lax.optimization_barrier(jnp.mean(center * center, axis=1, keepdims=True))
    normed = (center * lax.rsqrt(spread + 1e-06) * normalizer_multiplier).astype(jnp.bfloat16)
    preact = jnp.dot(normed, expanding_matrix, preferred_element_type=jnp.float32)
    hidden = jax.nn.gelu(preact, approximate=True).astype(jnp.bfloat16)
    slots = jnp.arange(IMG_PACK, dtype=jnp.int32)
    positions = jnp.arange(ROWS, dtype=jnp.int32)
    member = ((slot_ids[None, :] == slots[:, None]) & (positions[None, :] < count)).astype(jnp.float32)
    sizes = jnp.maximum(lax.optimization_barrier(jnp.sum(member, axis=1, keepdims=True)), 1.0)
    patch_mean = jnp.dot(member, values, precision=highest) / sizes
    hidden_mean = jnp.dot(member, hidden.astype(jnp.float32), precision=highest) / sizes
    return patch_mean + jnp.dot(hidden_mean, contracting_matrix.astype(jnp.float32), precision=highest)

def batch_derivatives(features, text_rows, image_ids, multiplier_coefficient, offset):
    image_unit = (features * lax.rsqrt(lax.optimization_barrier(jnp.sum(features * features, axis=1, keepdims=True)) + 1e-06)).astype(jnp.bfloat16)
    text_values = text_rows.astype(jnp.float32)
    text_unit = (text_values * lax.rsqrt(lax.optimization_barrier(jnp.sum(text_values * text_values, axis=1, keepdims=True)) + 1e-06)).astype(jnp.bfloat16)
    logits = multiplier_coefficient * jnp.dot(image_unit, text_unit.T, preferred_element_type=jnp.float32) + offset
    slots = jnp.arange(GROUP, dtype=jnp.int32)
    signs = jnp.where(image_ids[None, :] == slots[:, None], 1.0, -1.0).astype(jnp.float32)
    weights = (multiplier_coefficient * -signs * jax.nn.sigmoid(-signs * logits)).astype(jnp.bfloat16)
    image_grads = jnp.dot(weights, text_unit, preferred_element_type=jnp.float32)
    text_grads = jnp.dot(weights.T, image_unit, preferred_element_type=jnp.float32)
    return (image_grads, text_grads)

def reference(residual_tokens, patch_tallies, picture_assignment, normalizer_multiplier, expanding_matrix, contracting_matrix, sentence_vectors, described_picture_number, similarity_multiplier, additive_shift_term):
    packs = residual_tokens.reshape(GROUPS * PACKS_GROUP, ROWS, D)

    def one_pack(element_cursor):
        return pack_features(element_cursor[0], element_cursor[1], element_cursor[2], normalizer_multiplier, expanding_matrix, contracting_matrix)
    features = lax.map(one_pack, (packs, patch_tallies.reshape(GROUPS * PACKS_GROUP), picture_assignment.reshape(GROUPS * PACKS_GROUP, ROWS)))
    image_features = features.reshape(GROUPS, GROUP, D)

    def one_group(element_cursor):
        return batch_derivatives(element_cursor[0], element_cursor[1], element_cursor[2], similarity_multiplier[0], additive_shift_term[0])
    image_grads, text_grads = lax.map(one_group, (image_features, sentence_vectors, described_picture_number))
    return (image_features, image_grads, text_grads)
```

```python
import numpy as np
import jax
import jax.numpy as jnp
from jax import lax
from jax.experimental import pallas as pl
from jax.experimental.pallas import tpu as pltpu
from jax.sharding import PartitionSpec as P

MESH = pl.DeviceIdType.MESH
F32 = jnp.float32
BF16 = jnp.bfloat16
D = 1152
ROWS = 640
PIECE = 36
SET = 4 * PIECE
LANES = 128
HOPS = (1, -1, 2)
NT = (((1,), (1,)), ((), ()))


def column_origin():
    out = np.zeros((1, D), np.int32)
    for x in range(2):
        for z in range(16):
            k, rho = z // 4, z % 4
            at = SET * (rho * 2 + x) + PIECE * k
            out[0, at : at + PIECE] = PIECE * (x * 16 + z) + np.arange(PIECE)
    return out


def gelu(u):
    return 0.5 * u * (1.0 + jnp.tanh(0.7978845608028654 * (u + 0.044715 * (u * u * u))))


def two_bands(values):
    return jnp.concatenate([values[:, :640], values[:, 640:]], axis=0).astype(BF16)


def kernel(
    x_ref,
    count_ref,
    slot_ref,
    gain_ref,
    w1_ref,
    w2_ref,
    text_ref,
    ids_ref,
    mult_ref,
    shift_ref,
    origin_ref,
    features_out,
    image_out,
    text_out,
    pieces,
    w1,
    w2,
    perm,
    normed,
    member,
    texts,
    units,
    pooled,
    pooled_in,
    window,
    partial,
    returned,
    send_sem,
    recv_sem,
):
    blk, dp, mp = lax.axis_index("blk"), lax.axis_index("dp"), lax.axis_index("mp")
    y, c = lax.div(blk, 2), lax.rem(blk, 2)
    xl, z = lax.div(dp, 16), lax.rem(dp, 16)
    rho, k0 = lax.rem(z, 4), lax.div(z, 4)

    def dev(dy=0, dz=0, yy=None, cc=None, xx=None, mm=None):
        yy = lax.rem(y + dy + 8, 4) if yy is None else yy
        zz = lax.rem(z + dz + 32, 16)
        cc = c if cc is None else cc
        xx = xl if xx is None else xx
        mm = mp if mm is None else mm
        return {"blk": yy * 2 + cc, "dp": xx * 16 + zz, "mp": mm}

    def u_dev(off):
        return dev(dy=off * c, dz=off * (1 - c))

    def v_dev(off):
        return dev(dy=off * (1 - c), dz=off * c)

    started = []
    channels = [0]

    def send(src, dst, where, when=None):
        ch = channels[0]
        channels[0] += 1
        copy = pltpu.make_async_remote_copy(
            src_ref=src,
            dst_ref=dst,
            send_sem=send_sem.at[ch],
            recv_sem=recv_sem.at[ch],
            device_id=where,
            device_id_type=MESH,
        )
        if when is None:
            copy.start()
        else:
            pl.when(when)(copy.start)
        started.append((copy, when))
        return copy

    barrier = pltpu.get_barrier_semaphore()
    peers = [dev(dz=4), dev(dz=8), dev(dz=12)]
    for dx in (0, 1):
        for dz in (-2, -1, 0, 1, 2):
            for dm in (0, 1):
                if (dx, dz, dm) != (0, 0, 0):
                    peers.append(dev(dz=dz, xx=lax.rem(xl + dx, 2), mm=lax.rem(mp + dm, 2)))
    for dy in range(4):
        for dc in (0, 1):
            for dm in (0, 1):
                if (dy, dc) != (0, 0):
                    peers.append(dev(dy=dy, cc=lax.rem(c + dc, 2), mm=lax.rem(mp + dm, 2)))
    for peer in peers:
        pl.semaphore_signal(barrier, inc=1, device_id=peer, device_id_type=MESH)

    def two_tiles(a, b):
        both = [a.astype(F32), b.astype(F32), jnp.zeros((8, LANES), F32)]
        return jnp.concatenate(both, axis=0).astype(BF16)

    def tile_of(ref, index):
        return ref[:, pl.ds(pl.multiple_of(index * LANES, LANES), LANES)]

    def odd_tile(ref):
        part = ref[:, 2048:2152].astype(F32)
        return jnp.concatenate([part, jnp.zeros((PIECE, 24), F32)], axis=1)

    pieces[0, k0] = two_tiles(tile_of(w1_ref, c * 8 + y), tile_of(w1_ref, c * 8 + 4 + y))
    pieces[1, k0] = two_tiles(odd_tile(w1_ref), odd_tile(w2_ref))
    pieces[2, k0] = two_tiles(tile_of(w2_ref, c * 8 + y), tile_of(w2_ref, c * 8 + 4 + y))
    pl.semaphore_wait(barrier, len(peers))
    is_even = c == 0
    first = [
        [send(pieces.at[j, k0], pieces.at[j, k0], dev(dz=dz), is_even if j == 1 else None) for dz in (8, 4, 12)]
        for j in range(3)
    ]

    text = text_ref[...].astype(F32)
    text = text * lax.rsqrt(jnp.sum(text * text, axis=1, keepdims=True) + 1e-06)
    diagonal = lax.broadcasted_iota(jnp.int32, (4, 4), 0) == lax.broadcasted_iota(jnp.int32, (4, 4), 1)
    ids = jnp.sum(jnp.where(diagonal, jnp.broadcast_to(ids_ref[...], (4, 4)), 0).astype(F32), axis=1, keepdims=True)
    own_text = jnp.concatenate([text, jnp.broadcast_to(ids, (4, LANES))], axis=1)
    own_text = jnp.concatenate([own_text, jnp.zeros((4, D + LANES), F32)], axis=0)
    own_slot = blk * 2 + mp
    texts[own_slot] = two_bands(own_text)
    text_sends = []
    for dy in range(4):
        for dc in (0, 1):
            for dm in (0, 1):
                if (dy, dc, dm) != (0, 0, 0):
                    where = dev(dy=dy, cc=lax.rem(c + dc, 2), mm=lax.rem(mp + dm, 2))
                    text_sends.append(send(texts.at[own_slot], texts.at[own_slot], where))
    positions = lax.broadcasted_iota(jnp.int32, (8, ROWS), 1)
    slots = lax.broadcasted_iota(jnp.int32, (8, ROWS), 0)
    is_member = (jnp.broadcast_to(slot_ref[...], (8, ROWS)) == slots) & (positions < count_ref[0])
    own_member = jnp.where(is_member, 1.0, 0.0).astype(F32)
    member[c] = own_member
    core = dev(cc=1 - c)
    member_send = send(member.at[c], member.at[c], core)
    own_sizes = jnp.maximum(jnp.sum(own_member, axis=1, keepdims=True), 1.0)

    chunk = 128

    def perm_step(i, _):
        rows = pl.ds(pl.multiple_of(i * chunk, chunk), chunk)
        origin = lax.broadcasted_iota(jnp.int32, (chunk, D), 0) + i * chunk
        perm[rows, :] = jnp.where(origin == origin_ref[...], 1.0, 0.0).astype(BF16)
        return 0

    lax.fori_loop(0, D // chunk, perm_step, 0)

    def norm_step(i, _):
        rows = pl.ds(pl.multiple_of(i * chunk, chunk), chunk)
        values = x_ref[rows, :].astype(F32)
        center = values - jnp.mean(values, axis=1, keepdims=True)
        spread = jnp.mean(center * center, axis=1, keepdims=True)
        scaled = (center * lax.rsqrt(spread + 1e-06) * gain_ref[...]).astype(BF16)
        normed[c, rows, :] = jnp.dot(scaled, perm[...], preferred_element_type=F32).astype(BF16)
        return 0

    lax.fori_loop(0, ROWS // chunk, norm_step, 0)
    normed_send = send(normed.at[c], normed.at[c], core)
    patch_mean = jnp.dot(own_member.astype(BF16), x_ref[...], preferred_element_type=F32) / own_sizes

    def rows_of(r, x=None):
        if x is None:
            return pl.ds(pl.multiple_of(r * 2 * SET, 16), 2 * SET)
        return pl.ds(pl.multiple_of((r * 2 + x) * SET, 16), SET)

    def place(a, o=0):
        yy = lax.rem(y + 8 - a * c - o * (1 - c), 4)
        rr = lax.rem(rho + 8 - a * (1 - c) - o * c, 4)
        return yy, rr

    def block(tile, rows):
        return w1.at[tile, rows]

    def push(ref, where, when=None):
        return send(ref, ref, where, when)

    def stacked(j, t):
        parts = [pieces[j, k].astype(F32)[PIECE * t : PIECE * (t + 1)] for k in range(4)]
        return jnp.concatenate(parts, axis=0).astype(BF16)

    partner = dev(xx=1 - xl)
    for copy in first[0]:
        copy.wait_recv()
    for t in range(2):
        w1[t * 4 + y, rows_of(rho, xl), :] = stacked(0, t)
    mine = block(y, rows_of(rho, xl))
    own1 = block(4 + y, rows_of(rho, xl))
    a1 = push(mine, partner)
    b1 = [push(own1, u_dev(o)) for o in HOPS]
    b2 = {(0, o): push(own1, v_dev(o)) for o in HOPS}
    b3 = [push(own1, partner)]

    a1.wait_recv()
    pair = block(y, rows_of(rho))
    a2 = [push(pair, u_dev(o)) for o in HOPS]
    a3 = [push(pair, v_dev(o)) for o in HOPS]

    for copy in first[1]:
        pl.when(is_even)(copy.wait_recv)

    @pl.when(is_even)
    def _():
        w1[8, rows_of(rho, xl), :] = stacked(1, 0)
        w2[16] = stacked(1, 1)

    odd1 = push(block(8, rows_of(rho, xl)), partner, is_even)
    for copy in first[2]:
        copy.wait_recv()
    for t in range(2):
        w2[c * 8 + y * 2 + t] = stacked(2, t)
    own2 = w2.at[pl.ds(c * 8 + y * 2, 2)]
    w2_sends = [push(own2, dev(dy=dy)) for dy in (1, 3, 2)]
    pl.when(is_even)(odd1.wait_recv)
    odd2 = [push(block(8, rows_of(rho)), dev(dz=o), is_even) for o in HOPS]

    for a, copy in zip(HOPS, b1):
        copy.wait_recv()
        yy, rr = place(a)
        ref = block(4 + yy, rows_of(rr, xl))
        for o in HOPS:
            b2[a, o] = push(ref, v_dev(o))
        b3.append(push(ref, partner))
    for a, copy in zip(HOPS, a2):
        copy.wait_recv()
        yy, rr = place(a)
        ref = block(yy, rows_of(rr))
        for o in HOPS:
            a3.append(push(ref, v_dev(o)))
    for (a, o), copy in list(b2.items()):
        copy.wait_recv()
        yy, rr = place(a, o)
        b3.append(push(block(4 + yy, rows_of(rr, xl)), partner))

    member_send.wait_recv()
    normed_send.wait_recv()

    def tile_work(first_tile, tiles):
        if tiles == 2:
            weights = jnp.concatenate([w1[first_tile], w1[first_tile + 1]], axis=1)
        else:
            weights = w1[first_tile]
        for q in range(2):
            hidden = gelu(jnp.dot(normed[q], weights, preferred_element_type=F32)).astype(BF16)
            sums = jnp.dot(member[q].astype(BF16), hidden, preferred_element_type=F32)
            sizes = jnp.maximum(jnp.sum(member[q], axis=1, keepdims=True), 1.0)
            for t in range(tiles):
                pooled[q, first_tile + t] = sums[:, LANES * t : LANES * (t + 1)] / sizes

    def pair_step(i, _):
        tile_work(2 * i, 2)
        return 0

    for copy in a3:
        copy.wait_recv()
    lax.fori_loop(0, 2, pair_step, 0)
    for copy in w2_sends:
        copy.wait_recv()
    half = w2.at[pl.ds(c * 8, 8)]
    w2_core = push(half, core)
    w2_odd = send(w2.at[16], w2.at[16], core, is_even)
    for copy in odd2:
        pl.when(is_even)(copy.wait_recv)
    pl.when(is_even)(lambda: tile_work(8, 1))

    @pl.when(c == 1)
    def _():
        pooled[:, 8] = jnp.zeros((2, 8, LANES), F32)

    for copy in b3:
        copy.wait_recv()
    lax.fori_loop(2, 4, pair_step, 0)

    pooled_send = send(pooled.at[1 - c], pooled_in, core)
    pooled_send.wait_recv()
    own = jnp.concatenate([pooled[c, t] for t in range(9)], axis=1)
    other = jnp.concatenate([pooled_in[t] for t in range(9)], axis=1)
    low = jnp.where(is_even, own, other)
    high = jnp.where(is_even, other, own)
    own_window = xl * 4
    window[own_window] = jnp.concatenate([low, high], axis=0).astype(BF16)
    window_sends = []
    for n, o in enumerate((0,) + HOPS):
        for dx in (0, 1):
            if (o, dx) == (0, 0):
                continue
            where = dev(dz=o, xx=lax.rem(xl + dx, 2))
            window_sends.append(send(window.at[own_window], window.at[own_window + n], where))
    w2_core.wait_recv()
    pl.when(c == 1)(w2_odd.wait_recv)
    order = [yy * 2 + t for t in range(2) for yy in range(4)]
    low2 = jnp.concatenate([w2[n] for n in order] + [w2[16]], axis=1)
    high2 = jnp.concatenate([w2[8 + n] for n in order], axis=1)
    for copy in window_sends:
        copy.wait_recv()
    gathered = window[...].astype(F32)
    low1 = gathered[:, :8].reshape(64, D).astype(BF16)
    high1 = gathered[:, 8:, :1024].reshape(64, 1024).astype(BF16)
    result = lax.dot_general(low1, low2, NT, preferred_element_type=F32)
    result = result + lax.dot_general(high1, high2, NT, preferred_element_type=F32)
    partial[...] = jnp.concatenate([result, jnp.zeros((64, 256 - SET), F32)], axis=1)
    my_set = mp * 8 + rho * 2 + xl
    returned_sends = []
    for n, o in enumerate((0,) + HOPS):
        for dx in (0, 1):
            xx = lax.rem(xl + dx, 2)
            rows = partial.at[pl.ds(pl.multiple_of((xx * 4 + n) * 8, 8), 8)]
            for dm in (0, 1):
                if (o, dx, dm) == (0, 0, 0):
                    continue
                where = dev(dz=-o, xx=xx, mm=lax.rem(mp + dm, 2))
                returned_sends.append(send(rows, returned.at[my_set], where))
    returned[my_set] = partial[pl.ds(pl.multiple_of(xl * 32, 8), 8), :]
    for copy in returned_sends:
        copy.wait_recv()
    sums = [returned[n] + returned[8 + n] for n in range(8)]
    columns = []
    for x in range(2):
        for zz in range(16):
            k, r = zz // 4, zz % 4
            columns.append(sums[r * 2 + x][:, PIECE * k : PIECE * (k + 1)])
    features = jnp.concatenate(columns, axis=1) + patch_mean
    features_out[...] = jnp.where(mp == 0, features[:4], features[4:])

    image_unit = features * lax.rsqrt(jnp.sum(features * features, axis=1, keepdims=True) + 1e-06)
    units[blk] = two_bands(jnp.concatenate([image_unit, jnp.zeros((8, LANES), F32)], axis=1))
    unit_sends = []
    for dy in range(4):
        for dc in (0, 1):
            if (dy, dc) != (0, 0):
                where = dev(dy=dy, cc=lax.rem(c + dc, 2))
                unit_sends.append(send(units.at[blk], units.at[blk], where))
    for copy in text_sends:
        copy.wait_recv()
    mult, shift = mult_ref[0], shift_ref[0]

    def weights_of(dots, same):
        signs = jnp.where(same, 1.0, -1.0).astype(F32)
        logits = mult * dots + shift
        return (mult * -signs * jax.nn.sigmoid(-signs * logits)).astype(BF16)

    captions = texts[...].astype(F32)
    all_text = jnp.concatenate([captions[:, :8], captions[:, 8:]], axis=2).reshape(128, D + LANES)
    id_column = all_text[:, D : D + 1]
    all_text = all_text[:, :D].astype(BF16)
    square = (128, 128)
    eye = lax.broadcasted_iota(jnp.int32, square, 0) == lax.broadcasted_iota(jnp.int32, square, 1)
    id_rows = jnp.dot(
        jnp.ones((8, 128), BF16), jnp.where(eye, id_column, 0.0).astype(BF16), preferred_element_type=F32
    )
    own_images = (lax.broadcasted_iota(jnp.int32, (8, 128), 0) + blk * 8).astype(F32)
    dots = lax.dot_general(image_unit.astype(BF16), all_text, NT, preferred_element_type=F32)
    image_weights = weights_of(dots, id_rows == own_images)
    image_grads = jnp.dot(image_weights, all_text, preferred_element_type=F32)
    image_out[...] = jnp.where(mp == 0, image_grads[:4], image_grads[4:])
    for copy in unit_sends:
        copy.wait_recv()
    bands = units[...].astype(F32)
    all_units = jnp.concatenate([bands[:, :8], bands[:, 8:, :512]], axis=2).reshape(64, D).astype(BF16)
    dots = lax.dot_general(own_text[:, :D].astype(BF16), all_units, NT, preferred_element_type=F32)
    image_ids = lax.broadcasted_iota(jnp.int32, (8, 64), 1).astype(F32)
    text_weights = weights_of(dots, own_text[:, D : D + 1] == image_ids)
    text_out[...] = jnp.dot(text_weights, all_units, preferred_element_type=F32)[:4]

    for copy, when in started:
        if when is None:
            copy.wait_send()
        else:
            pl.when(when)(copy.wait_send)


CHANNELS = 136


def per_device(x, tallies, slots, gain, w1, w2, texts, ids, mult, shift):
    vmem = pl.BlockSpec(memory_space=pltpu.VMEM)
    smem = pl.BlockSpec(memory_space=pltpu.SMEM)
    out = jax.ShapeDtypeStruct((4, D), F32)
    results = pl.pallas_call(
        kernel,
        out_shape=(out, out, out),
        in_specs=[vmem, smem, vmem, vmem, vmem, vmem, vmem, vmem, smem, smem, vmem],
        out_specs=(vmem, vmem, vmem),
        scratch_shapes=[
            pltpu.VMEM((3, 4, 80, LANES), BF16),
            pltpu.VMEM((9, D, LANES), BF16),
            pltpu.VMEM((17, SET, LANES), BF16),
            pltpu.VMEM((D, D), BF16),
            pltpu.VMEM((2, ROWS, D), BF16),
            pltpu.VMEM((2, 8, ROWS), F32),
            pltpu.VMEM((16, 16, 640), BF16),
            pltpu.VMEM((8, 16, 640), BF16),
            pltpu.VMEM((2, 9, 8, LANES), F32),
            pltpu.VMEM((9, 8, LANES), F32),
            pltpu.VMEM((8, 16, D), BF16),
            pltpu.VMEM((64, 256), F32),
            pltpu.VMEM((16, 8, 256), F32),
            pltpu.SemaphoreType.DMA((CHANNELS,)),
            pltpu.SemaphoreType.DMA((CHANNELS,)),
        ],
        compiler_params=pltpu.CompilerParams(
            collective_id=0, has_side_effects=True, vmem_limit_bytes=48 << 20
        ),
        name="siglip_step",
    )(
        x[0, 0],
        tallies[0],
        slots[0],
        gain[None],
        w1,
        w2.T,
        texts[0],
        ids,
        mult,
        shift,
        jnp.asarray(column_origin()),
    )
    return tuple(r[None] for r in results)


def solution(mesh):
    in_specs = (
        P("dp", "blk", None, None),
        P("dp", "blk"),
        P("dp", "blk", None),
        P(),
        P("dp", "mp"),
        P("mp", "dp"),
        P("dp", ("blk", "mp"), None),
        P("dp", ("blk", "mp")),
        P(),
        P(),
    )
    out_specs = (P("dp", ("blk", "mp"), None),) * 3
    return jax.shard_map(per_device, mesh=mesh, in_specs=in_specs, out_specs=out_specs, check_vma=False)
```

```python
import jax
import jax.numpy as jnp
from jax import lax
from jax.experimental import pallas as pl
from jax.experimental.pallas import tpu as pltpu
from jax.sharding import PartitionSpec as P

MESH = pl.DeviceIdType.MESH
F32 = jnp.float32
BF16 = jnp.bfloat16
D = 1152
ROWS = 640
PIECE = 36
SET = 4 * PIECE
LANES = 128
HOPS = (1, -1, 2)
SIDES = (1, -1)
PASSED = ((0, 1), (1, 1), (-1, -1), (2, -1))
NT = (((1,), (1,)), ((), ()))


def column_origin(shape):
    r = lax.broadcasted_iota(jnp.int32, shape, 1)
    group = (r * 29128) >> 22
    inside = r - group * SET
    k = (inside * 1821) >> 16
    return r + ((group & 1) * 16 + 4 * k + (group >> 1) - group * 4 - k) * PIECE


def gelu(u):
    return 0.5 * u * (1.0 + jnp.tanh(0.7978845608028654 * (u + 0.044715 * (u * u * u))))


def two_bands(values):
    return jnp.concatenate([values[:, :640], values[:, 640:]], axis=0).astype(BF16)


def kernel(
    x_hbm,
    count_ref,
    slot_hbm,
    gain_hbm,
    w1_hbm,
    w2_hbm,
    text_hbm,
    ids_hbm,
    mult_ref,
    shift_ref,
    features_out,
    image_out,
    text_out,
    x_ref,
    slot_ref,
    gain_ref,
    w1_ref,
    w2_ref,
    text_ref,
    ids_ref,
    pieces,
    w1,
    w2,
    perm,
    normed,
    member,
    half_texts,
    texts,
    units,
    pooled,
    window,
    partial,
    returned,
    load_sem,
    send_sem,
    recv_sem,
):
    loads = [
        pltpu.make_async_copy(src, dst, load_sem.at[n])
        for n, (src, dst) in enumerate(
            [
                (w1_hbm, w1_ref),
                (w2_hbm, w2_ref),
                (text_hbm, text_ref),
                (ids_hbm, ids_ref),
                (slot_hbm, slot_ref),
                (gain_hbm, gain_ref),
                (x_hbm, x_ref),
            ]
        )
    ]
    for load in loads:
        load.start()
    blk, dp, mp = lax.axis_index("blk"), lax.axis_index("dp"), lax.axis_index("mp")
    y, c = lax.div(blk, 2), lax.rem(blk, 2)
    xl, z = lax.div(dp, 16), lax.rem(dp, 16)
    rho, k0 = lax.rem(z, 4), lax.div(z, 4)

    def dev(dy=0, dz=0, yy=None, cc=None, xx=None, mm=None):
        yy = lax.rem(y + dy + 8, 4) if yy is None else yy
        zz = lax.rem(z + dz + 32, 16)
        cc = c if cc is None else cc
        xx = xl if xx is None else xx
        mm = mp if mm is None else mm
        return {"blk": yy * 2 + cc, "dp": xx * 16 + zz, "mp": mm}

    def u_dev(off):
        return dev(dy=off * c, dz=off * (1 - c))

    def v_dev(off):
        return dev(dy=off * (1 - c), dz=off * c)

    started = []
    channels = [0]

    def send(src, dst, where, when=None):
        ch = channels[0]
        channels[0] += 1
        copy = pltpu.make_async_remote_copy(
            src_ref=src,
            dst_ref=dst,
            send_sem=send_sem.at[ch],
            recv_sem=recv_sem.at[ch],
            device_id=where,
            device_id_type=MESH,
        )
        if when is None:
            copy.start()
        else:
            pl.when(when)(copy.start)
        started.append((copy, when))
        return copy

    barrier = pltpu.get_barrier_semaphore()
    peers = [dev(dz=4), dev(dz=12)]
    for dx in (0, 1):
        for dz in (-2, -1, 0, 1, 2):
            for dc, dm in ((0, 0), (0, 1), (1, 0)):
                if (dx, dz, dc, dm) != (0, 0, 0, 0):
                    xx, cc, mm = lax.rem(xl + dx, 2), lax.rem(c + dc, 2), lax.rem(mp + dm, 2)
                    peers.append(dev(dz=dz, xx=xx, cc=cc, mm=mm))
    for dy in (1, 2, 3):
        for dc in (0, 1):
            peers.append(dev(dy=dy, cc=lax.rem(c + dc, 2)))
    for peer in peers:
        pl.semaphore_signal(barrier, inc=1, device_id=peer, device_id_type=MESH)

    def two_tiles(a, b):
        both = [a.astype(F32), b.astype(F32), jnp.zeros((8, LANES), F32)]
        return jnp.concatenate(both, axis=0).astype(BF16)

    def tile_of(ref, index):
        return ref[:, pl.ds(pl.multiple_of(index * LANES, LANES), LANES)]

    def odd_tile(ref):
        part = ref[:, 2048:2152].astype(F32)
        return jnp.concatenate([part, jnp.zeros((PIECE, 24), F32)], axis=1)

    is_even = c == 0
    core = dev(cc=1 - c)
    partner = dev(xx=1 - xl)

    def push(ref, where, when=None):
        return send(ref, ref, where, when)

    def first_phase(j, when=None):
        return [push(pieces.at[j, k0], dev(dz=dz), when) for dz in (4, 12)]

    def first_onward(j, copies, when=None):
        for copy in copies:
            if when is None:
                copy.wait_recv()
            else:
                pl.when(when)(copy.wait_recv)
        return [
            push(pieces.at[j, lax.rem(k0 + 3, 4), pl.ds(0, 48)], dev(dz=4), when),
            push(pieces.at[j, lax.rem(k0 + 1, 4), pl.ds(48, 32)], dev(dz=12), when),
        ]

    loads[0].wait()
    pieces[0, k0] = two_tiles(tile_of(w1_ref, c * 8 + y), tile_of(w1_ref, c * 8 + 4 + y))
    pl.semaphore_wait(barrier, len(peers))
    first0 = first_phase(0)
    loads[1].wait()
    pieces[1, k0] = two_tiles(odd_tile(w1_ref), odd_tile(w2_ref))
    pieces[2, k0] = two_tiles(tile_of(w2_ref, c * 8 + y), tile_of(w2_ref, c * 8 + 4 + y))

    chunk = 128

    def perm_step(i, _):
        rows = pl.ds(pl.multiple_of(i * chunk, chunk), chunk)
        origin = lax.broadcasted_iota(jnp.int32, (chunk, D), 0) + i * chunk
        perm[rows, :] = jnp.where(origin == column_origin((chunk, D)), 1.0, 0.0).astype(BF16)
        return 0

    lax.fori_loop(0, D // chunk, perm_step, 0)
    onward0 = first_onward(0, first0)
    first1 = first_phase(1, is_even)
    first2 = first_phase(2)
    for load in loads[2:]:
        load.wait()
    gain = gain_ref[...].reshape(1, D)
    band = 320

    def norm_step(i, _):
        rows = pl.ds(pl.multiple_of(i * band, band), band)
        values = x_ref[rows, :].astype(F32)
        center = values - jnp.mean(values, axis=1, keepdims=True)
        spread = jnp.mean(center * center, axis=1, keepdims=True)
        scaled = (center * lax.rsqrt(spread + 1e-06) * gain).astype(BF16)
        normed[c, rows, :] = jnp.dot(scaled, perm[...], preferred_element_type=F32).astype(BF16)
        return 0

    lax.fori_loop(0, ROWS // band, norm_step, 0)
    normed_send = push(normed.at[c], core)

    def rows_of(r, x=None):
        if x is None:
            return pl.ds(pl.multiple_of(r * 2 * SET, 16), 2 * SET)
        return pl.ds(pl.multiple_of((r * 2 + x) * SET, 16), SET)

    def place(a, o=0):
        yy = lax.rem(y + 8 - a * c - o * (1 - c), 4)
        rr = lax.rem(rho + 8 - a * (1 - c) - o * c, 4)
        return yy, rr

    def block(group, where, x=None):
        yy, rr = where
        return w1.at[group * 4 + yy, rows_of(rr, x)]

    def stacked(j, t):
        parts = [pieces[j, k].astype(F32)[PIECE * t : PIECE * (t + 1)] for k in range(4)]
        return jnp.concatenate(parts, axis=0).astype(BF16)

    along = {}

    def both_ways(group, a):
        ref = block(group, place(a))
        along[group, a, 1] = push(ref, v_dev(1))
        along[group, a, -1] = push(ref, v_dev(-1))

    for copy in onward0:
        copy.wait_recv()
    for t in range(2):
        w1[t * 4 + y, rows_of(rho, xl), :] = stacked(0, t)
    a1 = push(block(0, place(0), xl), partner)
    own1 = block(1, place(0), xl)
    across = {0: push(own1, partner)}
    b1 = {o: push(own1, u_dev(o)) for o in SIDES}
    onward1 = first_onward(1, first1, is_even)
    onward2 = first_onward(2, first2)

    text = text_ref[...].astype(F32)
    text = text * lax.rsqrt(jnp.sum(text * text, axis=1, keepdims=True) + 1e-06)
    diagonal = lax.broadcasted_iota(jnp.int32, (4, 4), 0) == lax.broadcasted_iota(jnp.int32, (4, 4), 1)
    ids = jnp.sum(jnp.where(diagonal, jnp.broadcast_to(ids_ref[...], (4, 4)), 0).astype(F32), axis=1, keepdims=True)
    text_rows = jnp.concatenate([text, jnp.broadcast_to(ids, (4, LANES))], axis=1)
    blank = jnp.zeros((4, D + LANES), F32)
    own_text = jnp.concatenate([text_rows, blank], axis=0)
    placed_text = jnp.where(mp == 0, own_text, jnp.concatenate([blank, text_rows], axis=0))
    half_texts[mp] = two_bands(placed_text)
    half_send = push(half_texts.at[mp], dev(mm=1 - mp))
    positions = lax.broadcasted_iota(jnp.int32, (8, ROWS), 1)
    slots = lax.broadcasted_iota(jnp.int32, (8, ROWS), 0)
    is_member = (jnp.broadcast_to(slot_ref[...], (8, ROWS)) == slots) & (positions < count_ref[0])
    own_member = jnp.where(is_member, 1.0, 0.0).astype(F32)
    member[c] = own_member
    member_send = push(member.at[c], core)
    own_sizes = jnp.maximum(jnp.sum(own_member, axis=1, keepdims=True), 1.0)

    def onward_pair(ref_at, copies, where, when=None):
        out = []
        for o in SIDES:
            if when is None:
                copies[o].wait_recv()
            else:
                pl.when(when)(copies[o].wait_recv)
            out.append(push(ref_at(o, 0 if o == 1 else 1), where(o), when))
        return out

    a1.wait_recv()
    pair = block(0, place(0))
    a2 = {o: push(pair, u_dev(o)) for o in SIDES}
    both_ways(0, 0)
    across[0].wait_recv()
    both_ways(1, 0)
    b2 = []
    for o in SIDES:
        b1[o].wait_recv()
        across[o] = push(block(1, place(o), xl), partner)
        yy, rr = place(o)
        start = (rr * 2 + xl) * SET + (0 if o == 1 else 80)
        part = w1.at[4 + yy, pl.ds(pl.multiple_of(start, 16), 80 if o == 1 else 64)]
        b2.append(push(part, u_dev(o)))
    a3 = onward_pair(lambda o, x: block(0, place(o), x), a2, u_dev)
    for o in SIDES:
        both_ways(0, o)
    for copy in onward1:
        pl.when(is_even)(copy.wait_recv)

    @pl.when(is_even)
    def _():
        w1[8, rows_of(rho, xl), :] = stacked(1, 0)
        w2[16] = stacked(1, 1)

    @pl.when(c == 1)
    def _():
        w1[8] = jnp.zeros((D, LANES), BF16)

    odd1 = push(w1.at[8, rows_of(rho, xl)], partner, is_even)
    for o in SIDES:
        across[o].wait_recv()
        both_ways(1, o)
    for copy in b2:
        copy.wait_recv()
    across[2] = push(block(1, place(2), xl), partner)
    for copy in a3:
        copy.wait_recv()
    both_ways(0, 2)
    for copy in onward2:
        copy.wait_recv()
    for t in range(2):
        w2[c * 8 + y * 2 + t] = stacked(2, t)
    own2 = w2.at[pl.ds(c * 8 + y * 2, 2)]
    pl.when(is_even)(odd1.wait_recv)
    odd2 = {o: push(w1.at[8, rows_of(rho)], dev(dz=o), is_even) for o in SIDES}
    patch_mean = jnp.dot(own_member.astype(BF16), x_ref[...], preferred_element_type=F32) / own_sizes

    def pass_on(group, a, o):
        along[group, a, o].wait_recv()
        along[group, a, 2 * o] = push(block(group, place(a, o)), v_dev(o))

    pass_on(0, *PASSED[0])
    pass_on(1, *PASSED[0])
    across[2].wait_recv()
    both_ways(1, 2)
    w2_sides = {o: push(own2, dev(dy=o)) for o in SIDES}
    for a, o in PASSED[1:]:
        pass_on(0, a, o)
    odd3 = onward_pair(lambda o, x: w1.at[8, rows_of(lax.rem(rho + 4 - o, 4), x)], odd2, lambda o: dev(dz=o), is_even)
    for a, o in PASSED[1:]:
        pass_on(1, a, o)
    w2_far = onward_pair(lambda o, x: w2.at[c * 8 + lax.rem(y + 4 - o, 4) * 2 + x], w2_sides, lambda o: dev(dy=o))
    half_send.wait_recv()
    texts[blk] = half_texts[0] + half_texts[1]
    text_sides = {o: push(texts.at[blk], dev(dy=o)) for o in SIDES}
    text_sends = [push(texts.at[blk], core)]

    def text_of(dy):
        return texts.at[lax.rem(y + dy + 4, 4) * 2 + c]

    member_send.wait_recv()
    normed_send.wait_recv()
    nothing = jnp.zeros((8, ROWS), F32)
    members = [
        jnp.concatenate([member[0], nothing], axis=0).astype(BF16),
        jnp.concatenate([nothing, member[1]], axis=0).astype(BF16),
    ]
    sizes = [jnp.maximum(jnp.sum(member[q], axis=1, keepdims=True), 1.0) for q in range(2)]

    def tile_work(tiles):
        weights = jnp.concatenate([w1[t] for t in tiles], axis=1)
        sums = jnp.zeros((16, LANES * len(tiles)), F32)
        for q in range(2):
            hidden = gelu(jnp.dot(normed[q], weights, preferred_element_type=F32)).astype(BF16)
            sums = sums + jnp.dot(members[q], hidden, preferred_element_type=F32)
        return sums / jnp.concatenate(sizes, axis=0)

    for copy in [copy for key, copy in along.items() if key[0] == 0 and (key[1], key[2]) not in PASSED]:
        copy.wait_recv()
    for copy in odd3:
        pl.when(is_even)(copy.wait_recv)
    low_sums = tile_work((0, 1, 2, 3, 8))
    for copy in w2_far:
        copy.wait_recv()
    for o in SIDES:
        text_sides[o].wait_recv()
    turn = 1 - 2 * c
    text_far = push(texts.at[lax.rem(y + 4 - turn, 4) * 2 + c], dev(dy=turn))
    text_sends += [push(text_of(o), core) for o in SIDES]
    w2_core = push(w2.at[pl.ds(c * 8, 8)], core)
    w2_odd = push(w2.at[16], core, is_even)
    for copy in [copy for key, copy in along.items() if key[0] == 1 and (key[1], key[2]) not in PASSED]:
        copy.wait_recv()
    high_sums = tile_work((4, 5, 6, 7))

    both_sums = jnp.concatenate([low_sums[:, :512], high_sums, low_sums[:, 512:], jnp.zeros((16, LANES), F32)], axis=1)
    for q in range(2):
        pooled[q] = two_bands(both_sums[8 * q : 8 * q + 8])
    own_window = xl * 4
    window[own_window, c] = pooled[c]
    window_sends = []
    for n, o in enumerate((0,) + HOPS):
        for dx in (0, 1):
            for dc in (0, 1):
                if (o, dx, dc) == (0, 0, 0):
                    continue
                cc = lax.rem(c + dc, 2)
                where = dev(dz=o, xx=lax.rem(xl + dx, 2), cc=cc)
                window_sends.append(send(pooled.at[cc], window.at[own_window + n, c], where))
    text_far.wait_recv()
    text_sends.append(push(text_of(2), core))
    w2_core.wait_recv()
    pl.when(c == 1)(w2_odd.wait_recv)
    order = [yy * 2 + t for t in range(2) for yy in range(4)]
    low2 = jnp.concatenate([w2[n] for n in order] + [w2[16]], axis=1)
    high2 = jnp.concatenate([w2[8 + n] for n in order], axis=1)
    for copy in window_sends:
        copy.wait_recv()
    gathered = window[...].astype(F32)
    low1 = jnp.concatenate([gathered[:, 0, :8], gathered[:, 0, 8:, :512]], axis=2).reshape(64, D).astype(BF16)
    high1 = jnp.concatenate([gathered[:, 1, :8], gathered[:, 1, 8:, :384]], axis=2).reshape(64, 1024).astype(BF16)
    result = lax.dot_general(low1, low2, NT, preferred_element_type=F32)
    result = result + lax.dot_general(high1, high2, NT, preferred_element_type=F32)
    partial[...] = jnp.concatenate([result, jnp.zeros((64, 256 - SET), F32)], axis=1)
    my_set = mp * 8 + rho * 2 + xl
    returned_sends = []
    for n, o in enumerate((0,) + HOPS):
        for dx in (0, 1):
            xx = lax.rem(xl + dx, 2)
            rows = partial.at[pl.ds(pl.multiple_of((xx * 4 + n) * 8, 8), 8)]
            for dm in (0, 1):
                if (o, dx, dm) == (0, 0, 0):
                    continue
                where = dev(dz=-o, xx=xx, mm=lax.rem(mp + dm, 2))
                returned_sends.append(send(rows, returned.at[my_set], where))
    returned[my_set] = partial[pl.ds(pl.multiple_of(xl * 32, 8), 8), :]
    for copy in returned_sends:
        copy.wait_recv()
    sums = [returned[n] + returned[8 + n] for n in range(8)]
    columns = []
    for x in range(2):
        for zz in range(16):
            k, r = zz // 4, zz % 4
            columns.append(sums[r * 2 + x][:, PIECE * k : PIECE * (k + 1)])
    features = jnp.concatenate(columns, axis=1) + patch_mean
    features_out[...] = jnp.where(mp == 0, features[:4], features[4:])

    image_unit = features * lax.rsqrt(jnp.sum(features * features, axis=1, keepdims=True) + 1e-06)
    units[blk] = two_bands(jnp.concatenate([image_unit, jnp.zeros((8, LANES), F32)], axis=1))
    unit_sends = []
    for dy in range(4):
        for dc in (0, 1):
            if (dy, dc) != (0, 0):
                where = dev(dy=dy, cc=lax.rem(c + dc, 2))
                unit_sends.append(send(units.at[blk], units.at[blk], where))
    for copy in text_sends:
        copy.wait_recv()
    mult, shift = mult_ref[0], shift_ref[0]

    def weights_of(dots, same):
        signs = jnp.where(same, 1.0, -1.0).astype(F32)
        logits = mult * dots + shift
        return (mult * -signs * jax.nn.sigmoid(-signs * logits)).astype(BF16)

    captions = texts[...].astype(F32)
    all_text = jnp.concatenate([captions[:, :8], captions[:, 8:]], axis=2).reshape(64, D + LANES)
    id_column = all_text[:, D : D + 1]
    all_text = all_text[:, :D].astype(BF16)
    square = (64, 64)
    eye = lax.broadcasted_iota(jnp.int32, square, 0) == lax.broadcasted_iota(jnp.int32, square, 1)
    id_rows = jnp.dot(
        jnp.ones((8, 64), BF16), jnp.where(eye, id_column, 0.0).astype(BF16), preferred_element_type=F32
    )
    own_images = (lax.broadcasted_iota(jnp.int32, (8, 64), 0) + blk * 8).astype(F32)
    dots = lax.dot_general(image_unit.astype(BF16), all_text, NT, preferred_element_type=F32)
    image_weights = weights_of(dots, id_rows == own_images)
    image_grads = jnp.dot(image_weights, all_text, preferred_element_type=F32)
    image_out[...] = jnp.where(mp == 0, image_grads[:4], image_grads[4:])
    for copy in unit_sends:
        copy.wait_recv()
    bands = units[...].astype(F32)
    all_units = jnp.concatenate([bands[:, :8], bands[:, 8:, :512]], axis=2).reshape(64, D).astype(BF16)
    dots = lax.dot_general(own_text[:, :D].astype(BF16), all_units, NT, preferred_element_type=F32)
    image_ids = lax.broadcasted_iota(jnp.int32, (8, 64), 1).astype(F32)
    text_weights = weights_of(dots, own_text[:, D : D + 1] == image_ids)
    text_out[...] = jnp.dot(text_weights, all_units, preferred_element_type=F32)[:4]

    for copy, when in started:
        if when is None:
            copy.wait_send()
        else:
            pl.when(when)(copy.wait_send)


CHANNELS = 136


def per_device(x, tallies, slots, gain, w1, w2, texts, ids, mult, shift):
    vmem = pl.BlockSpec(memory_space=pltpu.VMEM)
    smem = pl.BlockSpec(memory_space=pltpu.SMEM)
    hbm = pl.BlockSpec(memory_space=pltpu.HBM)
    out = jax.ShapeDtypeStruct((4, D), F32)
    results = pl.pallas_call(
        kernel,
        out_shape=(out, out, out),
        in_specs=[hbm, smem, hbm, hbm, hbm, hbm, hbm, hbm, smem, smem],
        out_specs=(vmem, vmem, vmem),
        scratch_shapes=[
            pltpu.VMEM((ROWS, D), BF16),
            pltpu.VMEM((1, ROWS), jnp.int32),
            pltpu.VMEM((D,), F32),
            pltpu.VMEM((PIECE, 2152), BF16),
            pltpu.VMEM((PIECE, 2152), BF16),
            pltpu.VMEM((4, D), BF16),
            pltpu.VMEM((1, 4), jnp.int32),
            pltpu.VMEM((3, 4, 80, LANES), BF16),
            pltpu.VMEM((9, D, LANES), BF16),
            pltpu.VMEM((17, SET, LANES), BF16),
            pltpu.VMEM((D, D), BF16),
            pltpu.VMEM((2, ROWS, D), BF16),
            pltpu.VMEM((2, 8, ROWS), F32),
            pltpu.VMEM((2, 16, 640), BF16),
            pltpu.VMEM((8, 16, 640), BF16),
            pltpu.VMEM((8, 16, 640), BF16),
            pltpu.VMEM((2, 16, 640), BF16),
            pltpu.VMEM((8, 2, 16, 640), BF16),
            pltpu.VMEM((64, 256), F32),
            pltpu.VMEM((16, 8, 256), F32),
            pltpu.SemaphoreType.DMA((7,)),
            pltpu.SemaphoreType.DMA((CHANNELS,)),
            pltpu.SemaphoreType.DMA((CHANNELS,)),
        ],
        compiler_params=pltpu.CompilerParams(
            collective_id=0, has_side_effects=True, vmem_limit_bytes=62 << 20
        ),
        name="siglip_step",
    )(
        x[0, 0],
        tallies[0],
        slots[0],
        gain,
        w1,
        w2.T,
        texts[0],
        ids,
        mult,
        shift,
    )
    return tuple(r[None] for r in results)


def solution(mesh):
    in_specs = (
        P("dp", "blk", None, None),
        P("dp", "blk"),
        P("dp", "blk", None),
        P(),
        P("dp", "mp"),
        P("mp", "dp"),
        P("dp", ("blk", "mp"), None),
        P("dp", ("blk", "mp")),
        P(),
        P(),
    )
    out_specs = (P("dp", ("blk", "mp"), None),) * 3
    return jax.shard_map(per_device, mesh=mesh, in_specs=in_specs, out_specs=out_specs, check_vma=False)
```

```python
import jax
import jax.numpy as jnp
from jax import lax
from jax.experimental import pallas as pl
from jax.experimental.pallas import tpu as pltpu
from jax.sharding import PartitionSpec as P

MESH = pl.DeviceIdType.MESH
F32 = jnp.float32
BF16 = jnp.bfloat16
D = 1152
ROWS = 640
PIECE = 36
SET = 4 * PIECE
LANES = 128
SIDES = (1, -1)
PASSED = ((0, 1), (1, 1), (-1, -1), (2, -1))
NT = (((1,), (1,)), ((), ()))


def column_origin(shape):
    r = lax.broadcasted_iota(jnp.int32, shape, 1)
    group = (r * 29128) >> 22
    inside = r - group * SET
    k = (inside * 1821) >> 16
    return r + ((group & 1) * 16 + 4 * k + (group >> 1) - group * 4 - k) * PIECE


def gelu(u):
    return 0.5 * u * (1.0 + jnp.tanh(0.7978845608028654 * (u + 0.044715 * (u * u * u))))


def two_bands(values):
    return jnp.concatenate([values[:, :640], values[:, 640:]], axis=0).astype(BF16)


def kernel(
    x_hbm,
    count_ref,
    slot_hbm,
    gain_hbm,
    w1_hbm,
    w2_hbm,
    text_hbm,
    ids_hbm,
    mult_ref,
    shift_ref,
    features_out,
    image_out,
    text_out,
    x_ref,
    slot_ref,
    gain_ref,
    w1_ref,
    w2_ref,
    text_ref,
    ids_ref,
    pieces,
    w1,
    w2,
    perm,
    normed,
    member,
    half_texts,
    texts,
    units,
    pooled_low,
    pooled_high,
    window_low,
    window_high,
    partial,
    returned,
    load_sem,
    send_sem,
    recv_sem,
):
    loads = [
        pltpu.make_async_copy(src, dst, load_sem.at[n])
        for n, (src, dst) in enumerate(
            [
                (w1_hbm, w1_ref),
                (w2_hbm, w2_ref),
                (text_hbm, text_ref),
                (ids_hbm, ids_ref),
                (slot_hbm, slot_ref),
                (gain_hbm, gain_ref),
                (x_hbm, x_ref),
            ]
        )
    ]
    for load in loads[:6]:
        load.start()
    blk, dp, mp = lax.axis_index("blk"), lax.axis_index("dp"), lax.axis_index("mp")
    y, c = lax.div(blk, 2), lax.rem(blk, 2)
    xl, z = lax.div(dp, 16), lax.rem(dp, 16)
    rho, k0 = lax.rem(z, 4), lax.div(z, 4)

    def dev(dy=0, dz=0, yy=None, cc=None, xx=None, mm=None):
        yy = lax.rem(y + dy + 8, 4) if yy is None else yy
        zz = lax.rem(z + dz + 32, 16)
        cc = c if cc is None else cc
        xx = xl if xx is None else xx
        mm = mp if mm is None else mm
        return {"blk": yy * 2 + cc, "dp": xx * 16 + zz, "mp": mm}

    def u_dev(off):
        return dev(dy=off * c, dz=off * (1 - c))

    def v_dev(off):
        return dev(dy=off * (1 - c), dz=off * c)

    started = []
    channels = [0]

    def send(src, dst, where, when=None):
        ch = channels[0]
        channels[0] += 1
        copy = pltpu.make_async_remote_copy(
            src_ref=src,
            dst_ref=dst,
            send_sem=send_sem.at[ch],
            recv_sem=recv_sem.at[ch],
            device_id=where,
            device_id_type=MESH,
        )
        if when is None:
            copy.start()
        else:
            pl.when(when)(copy.start)
        started.append((copy, when))
        return copy

    drained = [0]

    def drain(end):
        for copy, when in started[drained[0] : end]:
            if when is None:
                copy.wait_send()
            else:
                pl.when(when)(copy.wait_send)
        drained[0] = end

    barrier = pltpu.get_barrier_semaphore()
    peers = [dev(dz=4), dev(dz=12)]
    for dx in (0, 1):
        for dz in (-2, -1, 0, 1, 2):
            for dc, dm in ((0, 0), (0, 1), (1, 0)):
                if (dx, dz, dc, dm) != (0, 0, 0, 0):
                    xx, cc, mm = lax.rem(xl + dx, 2), lax.rem(c + dc, 2), lax.rem(mp + dm, 2)
                    peers.append(dev(dz=dz, xx=xx, cc=cc, mm=mm))
    for dy in (1, 2, 3):
        for dc in (0, 1):
            peers.append(dev(dy=dy, cc=lax.rem(c + dc, 2)))
    for peer in peers:
        pl.semaphore_signal(barrier, inc=1, device_id=peer, device_id_type=MESH)

    def two_tiles(a, b):
        both = [a.astype(F32), b.astype(F32), jnp.zeros((8, LANES), F32)]
        return jnp.concatenate(both, axis=0).astype(BF16)

    def tile_of(ref, index):
        return ref[:, pl.ds(pl.multiple_of(index * LANES, LANES), LANES)]

    def odd_tile(ref):
        part = ref[:, 2048:2152].astype(F32)
        return jnp.concatenate([part, jnp.zeros((PIECE, 24), F32)], axis=1)

    is_even = c == 0
    core = dev(cc=1 - c)
    partner = dev(xx=1 - xl)

    def push(ref, where, when=None):
        return send(ref, ref, where, when)

    def first_phase(j, when=None):
        return [push(pieces.at[j, k0], dev(dz=dz), when) for dz in (4, 12)]

    def first_onward(j, copies, when=None):
        for copy in copies:
            if when is None:
                copy.wait_recv()
            else:
                pl.when(when)(copy.wait_recv)
        return [
            push(pieces.at[j, lax.rem(k0 + 3, 4), pl.ds(0, 48)], dev(dz=4), when),
            push(pieces.at[j, lax.rem(k0 + 1, 4), pl.ds(48, 32)], dev(dz=12), when),
        ]

    chunk = 128

    def perm_step(i, _):
        rows = pl.ds(pl.multiple_of(i * chunk, chunk), chunk)
        origin = lax.broadcasted_iota(jnp.int32, (chunk, D), 0) + i * chunk
        perm[rows, :] = jnp.where(origin == column_origin((chunk, D)), 1.0, 0.0).astype(BF16)
        return 0

    loads[0].wait()
    loads[6].start()
    pieces[0, k0] = two_tiles(tile_of(w1_ref, c * 8 + y), tile_of(w1_ref, c * 8 + 4 + y))
    pl.semaphore_wait(barrier, len(peers))
    first0 = first_phase(0)
    loads[1].wait()
    pieces[1, k0] = two_tiles(odd_tile(w1_ref), odd_tile(w2_ref))
    pieces[2, k0] = two_tiles(tile_of(w2_ref, c * 8 + y), tile_of(w2_ref, c * 8 + 4 + y))
    first1 = first_phase(1, is_even)
    first2 = first_phase(2)
    lax.fori_loop(0, D // chunk, perm_step, 0)
    for load in loads[2:]:
        load.wait()
    gain = gain_ref[...].reshape(1, D)
    band = ROWS // 2

    def normalise(i):
        rows = pl.ds(i * band, band)
        values = x_ref[rows, :].astype(F32)
        center = values - jnp.mean(values, axis=1, keepdims=True)
        spread = jnp.mean(center * center, axis=1, keepdims=True)
        scaled = (center * lax.rsqrt(spread + 1e-06) * gain).astype(BF16)
        normed[c, rows, :] = jnp.dot(scaled, perm[...], preferred_element_type=F32).astype(BF16)

    normalise(0)
    onward0 = first_onward(0, first0)
    onward1 = first_onward(1, first1, is_even)
    onward2 = first_onward(2, first2)
    normalise(1)
    normed_send = push(normed.at[c], core)

    def rows_of(r, x=None):
        if x is None:
            return pl.ds(pl.multiple_of(r * 2 * SET, 16), 2 * SET)
        return pl.ds(pl.multiple_of((r * 2 + x) * SET, 16), SET)

    def place(a, o=0):
        yy = lax.rem(y + 8 - a * c - o * (1 - c), 4)
        rr = lax.rem(rho + 8 - a * (1 - c) - o * c, 4)
        return yy, rr

    def block(group, where, x=None):
        yy, rr = where
        return w1.at[group * 4 + yy, rows_of(rr, x)]

    def stacked(j, t):
        parts = [pieces[j, k].astype(F32)[PIECE * t : PIECE * (t + 1)] for k in range(4)]
        return jnp.concatenate(parts, axis=0).astype(BF16)

    along = {}

    def both_ways(group, a):
        ref = block(group, place(a))
        along[group, a, 1] = push(ref, v_dev(1))
        along[group, a, -1] = push(ref, v_dev(-1))

    for copy in onward0:
        copy.wait_recv()
    for t in range(2):
        w1[t * 4 + y, rows_of(rho, xl), :] = stacked(0, t)
    a1 = push(block(0, place(0), xl), partner)
    own1 = block(1, place(0), xl)
    across = {0: push(own1, partner)}
    b1 = {o: push(own1, u_dev(o)) for o in (1, -1, -2)}

    text = text_ref[...].astype(F32)
    text = text * lax.rsqrt(jnp.sum(text * text, axis=1, keepdims=True) + 1e-06)
    diagonal = lax.broadcasted_iota(jnp.int32, (4, 4), 0) == lax.broadcasted_iota(jnp.int32, (4, 4), 1)
    ids = jnp.sum(jnp.where(diagonal, jnp.broadcast_to(ids_ref[...], (4, 4)), 0).astype(F32), axis=1, keepdims=True)
    text_rows = jnp.concatenate([text, jnp.broadcast_to(ids, (4, LANES))], axis=1)
    blank = jnp.zeros((4, D + LANES), F32)
    own_text = jnp.concatenate([text_rows, blank], axis=0)
    placed_text = jnp.where(mp == 0, own_text, jnp.concatenate([blank, text_rows], axis=0))
    half_texts[mp] = two_bands(placed_text)
    half_send = push(half_texts.at[mp], dev(mm=1 - mp))
    positions = lax.broadcasted_iota(jnp.int32, (8, ROWS), 1)
    slots = lax.broadcasted_iota(jnp.int32, (8, ROWS), 0)
    is_member = (jnp.broadcast_to(slot_ref[...], (8, ROWS)) == slots) & (positions < count_ref[0])
    own_member = jnp.where(is_member, 1.0, 0.0).astype(F32)
    member[c] = own_member
    member_send = push(member.at[c], core)
    own_sizes = jnp.maximum(jnp.sum(own_member, axis=1, keepdims=True), 1.0)

    def onward_pair(ref_at, copies, where, when=None):
        out = []
        for o in SIDES:
            if when is None:
                copies[o].wait_recv()
            else:
                pl.when(when)(copies[o].wait_recv)
            out.append(push(ref_at(o, 0 if o == 1 else 1), where(o), when))
        return out

    def onward_pair(ref_at, copies, where, when=None):
        out = []
        for o in SIDES:
            if when is None:
                copies[o].wait_recv()
            else:
                pl.when(when)(copies[o].wait_recv)
            out.append(push(ref_at(o, 0 if o == 1 else 1), where(o), when))
        return out

    def pass_on(group, a, o):
        along[group, a, o].wait_recv()
        along[group, a, 2 * o] = push(block(group, place(a, o)), v_dev(o))

    last = []

    def finish(a, o):
        last.append(push(block(1, place(a, o), xl), partner))

    def onward_pair(ref_at, copies, where, when=None):
        out = []
        for o in SIDES:
            if when is None:
                copies[o].wait_recv()
            else:
                pl.when(when)(copies[o].wait_recv)
            out.append(push(ref_at(o, 0 if o == 1 else 1), where(o), when))
        return out

    def pass_on(group, a, o):
        along[group, a, o].wait_recv()
        along[group, a, 2 * o] = push(block(group, place(a, o)), v_dev(o))

    last = []

    def finish(a, o):
        last.append(push(block(1, place(a, o), xl), partner))

    a1.wait_recv()
    pair = block(0, place(0))
    a2 = {o: push(pair, u_dev(o)) for o in (1, -1, 2)}
    both_ways(0, 0)
    across[0].wait_recv()
    both_ways(1, 0)
    for o in SIDES:
        b1[o].wait_recv()
        single = block(1, place(o), xl)
        along[1, o, 1] = push(single, v_dev(1))
        along[1, o, -1] = push(single, v_dev(-1))
        finish(o, 0)
    b1[-2].wait_recv()
    across[2] = push(block(1, place(2), xl), partner)
    for a in (1, -1, 2):
        a2[a].wait_recv()
        both_ways(0, a)
    for copy in onward1:
        pl.when(is_even)(copy.wait_recv)

    @pl.when(is_even)
    def _():
        w1[8, rows_of(rho, xl), :] = stacked(1, 0)
        w2[16] = stacked(1, 1)

    @pl.when(c == 1)
    def _():
        w1[8] = jnp.zeros((D, LANES), BF16)

    odd1 = push(w1.at[8, rows_of(rho, xl)], partner, is_even)
    pass_on(0, *PASSED[0])
    pass_on(1, *PASSED[0])
    for a in SIDES:
        for o in SIDES:
            along[1, a, o].wait_recv()
            if a == o:
                along[1, a, 2 * o] = push(block(1, place(a, o), xl), v_dev(o))
            finish(a, o)
    pl.when(is_even)(odd1.wait_recv)
    odd2 = {o: push(w1.at[8, rows_of(rho)], dev(dz=o), is_even) for o in SIDES}
    across[2].wait_recv()
    both_ways(1, 2)
    for a, o in PASSED[1:]:
        pass_on(0, a, o)
    for copy in onward2:
        copy.wait_recv()
    for t in range(2):
        w2[c * 8 + y * 2 + t] = stacked(2, t)
    own2 = w2.at[pl.ds(c * 8 + y * 2, 2)]
    w2_sides = {o: push(own2, dev(dy=o)) for o in SIDES}
    odd3 = onward_pair(lambda o, x: w1.at[8, rows_of(lax.rem(rho + 4 - o, 4), x)], odd2, lambda o: dev(dz=o), is_even)
    pass_on(1, *PASSED[3])
    for a in SIDES:
        along[1, a, 2 * a].wait_recv()
        finish(a, 2 * a)

    member_send.wait_recv()
    normed_send.wait_recv()
    nothing = jnp.zeros((8, ROWS), F32)
    members = [
        jnp.concatenate([member[0], nothing], axis=0).astype(BF16),
        jnp.concatenate([nothing, member[1]], axis=0).astype(BF16),
    ]
    sizes = [jnp.maximum(jnp.sum(member[q], axis=1, keepdims=True), 1.0) for q in range(2)]

    def tile_work(tiles):
        weights = jnp.concatenate([w1[t] for t in tiles], axis=1)
        sums = jnp.zeros((16, LANES * len(tiles)), F32)
        for q in range(2):
            hidden = gelu(jnp.dot(normed[q], weights, preferred_element_type=F32)).astype(BF16)
            sums = sums + jnp.dot(members[q], hidden, preferred_element_type=F32)
        return sums / jnp.concatenate(sizes, axis=0)

    own_window = xl * 4

    def reach(n, cc):
        return (0, 1, -1)[n] if n < 3 else 2 - 4 * cc

    def window_phase(sums, bands, pool, there):
        for q in range(2):
            own = sums[8 * q : 8 * q + 8]
            pool[q] = jnp.concatenate([own[:, :bands], own[:, bands:]], axis=0).astype(BF16)
        there[own_window, c] = pool[c]
        out = []
        for n in (3, 1, 2, 0):
            for dx in (0, 1):
                for dc in (0, 1):
                    if (n, dx, dc) == (0, 0, 0):
                        continue
                    cc = lax.rem(c + dc, 2)
                    where = dev(dz=reach(n, cc), xx=lax.rem(xl + dx, 2), cc=cc)
                    out.append(send(pool.at[cc], there.at[own_window + n, c], where))
        return out

    for key, copy in along.items():
        if key[0] == 0 and key[1:] not in PASSED:
            copy.wait_recv()
    low_sums = tile_work((0, 1, 2, 3))
    low_sends = window_phase(low_sums, 256, pooled_low, window_low)
    w2_far = onward_pair(lambda o, x: w2.at[c * 8 + lax.rem(y + 4 - o, 4) * 2 + x], w2_sides, lambda o: dev(dy=o))
    half_send.wait_recv()
    texts[blk] = half_texts[0] + half_texts[1]
    text_sides = {o: push(texts.at[blk], dev(dy=o)) for o in SIDES}
    text_sends = [push(texts.at[blk], core)]
    for copy in last:
        copy.wait_recv()
    for key, copy in along.items():
        if key[0] == 1 and key[1:] not in PASSED and (key[1] in (0, 2)):
            copy.wait_recv()
    for copy in odd3:
        pl.when(is_even)(copy.wait_recv)
    high_sums = tile_work((4, 5, 6, 7, 8))
    high_sums = jnp.concatenate([high_sums, jnp.zeros((16, LANES), F32)], axis=1)
    before_window = len(started)
    high_sends = window_phase(high_sums, 384, pooled_high, window_high)
    patch_mean = jnp.dot(own_member.astype(BF16), x_ref[...], preferred_element_type=F32) / own_sizes
    for o in SIDES:
        text_sides[o].wait_recv()
    turn = 1 - 2 * c
    text_far = push(texts.at[lax.rem(y + 4 - turn, 4) * 2 + c], dev(dy=turn))

    def text_of(dy):
        return texts.at[lax.rem(y + dy + 4, 4) * 2 + c]

    text_sends += [push(text_of(o), core) for o in SIDES]
    for copy in w2_far:
        copy.wait_recv()
    w2_core = push(w2.at[pl.ds(c * 8, 8)], core)
    w2_odd = push(w2.at[16], core, is_even)
    w2_core.wait_recv()
    pl.when(c == 1)(w2_odd.wait_recv)
    bands = []
    for tiles in ((0, 1, 4, 5, 6), (2, 3, 7, 8, 9)):
        parts = []
        for half in range(2):
            for n in tiles:
                if n < 8:
                    parts.append(w2[half * 8 + (n % 4) * 2 + n // 4])
                elif n == 8 and half == 0:
                    parts.append(w2[16])
                else:
                    parts.append(jnp.zeros((SET, LANES), BF16))
        bands.append(jnp.concatenate(parts, axis=1))
    drain(before_window)
    for copy in low_sends + high_sends:
        copy.wait_recv()
    parts = []
    for half in range(2):
        parts += [window_low[:, half].reshape(128, 256), window_high[:, half].reshape(128, 384)]
    gathered = jnp.concatenate(parts, axis=1)
    over = [lax.dot_general(gathered, band, NT, preferred_element_type=F32).reshape(8, 16, SET) for band in bands]
    result = (over[0][:, :8] + over[1][:, 8:]).reshape(64, SET)
    partial[...] = jnp.concatenate([result, jnp.zeros((64, 256 - SET), F32)], axis=1)
    before_returned = len(started)
    my_set = mp * 8 + rho * 2 + xl
    returned_sends = []
    for n in (3, 1, 2, 0):
        for dx in (0, 1):
            xx = lax.rem(xl + dx, 2)
            rows = partial.at[pl.ds(pl.multiple_of((xx * 4 + n) * 8, 8), 8)]
            for dm in (0, 1):
                if (n, dx, dm) == (0, 0, 0):
                    continue
                where = dev(dz=-reach(n, c), xx=xx, mm=lax.rem(mp + dm, 2))
                returned_sends.append(send(rows, returned.at[my_set], where))
    returned[my_set] = partial[pl.ds(pl.multiple_of(xl * 32, 8), 8), :]
    text_far.wait_recv()
    text_sends.append(push(text_of(2), core))
    drain(before_returned)
    for copy in returned_sends:
        copy.wait_recv()
    sums = [returned[n] + returned[8 + n] for n in range(8)]
    columns = []
    for x in range(2):
        for zz in range(16):
            k, r = zz // 4, zz % 4
            columns.append(sums[r * 2 + x][:, PIECE * k : PIECE * (k + 1)])
    features = jnp.concatenate(columns, axis=1) + patch_mean
    features_out[...] = jnp.where(mp == 0, features[:4], features[4:])

    image_unit = features * lax.rsqrt(jnp.sum(features * features, axis=1, keepdims=True) + 1e-06)
    units[blk] = two_bands(jnp.concatenate([image_unit, jnp.zeros((8, LANES), F32)], axis=1))
    before_units = len(started)
    unit_sends = []
    for dy in (2, 1, 3, 0):
        for dc in (1, 0):
            if (dy, dc) != (0, 0):
                where = dev(dy=dy, cc=lax.rem(c + dc, 2))
                unit_sends.append(send(units.at[blk], units.at[blk], where))
    for copy in text_sends:
        copy.wait_recv()
    mult, shift = mult_ref[0], shift_ref[0]

    def weights_of(dots, same):
        signs = jnp.where(same, 1.0, -1.0).astype(F32)
        logits = mult * dots + shift
        return (mult * -signs * jax.nn.sigmoid(-signs * logits)).astype(BF16)

    captions = texts[...].astype(F32)
    all_text = jnp.concatenate([captions[:, :8], captions[:, 8:]], axis=2).reshape(64, D + LANES)
    id_column = all_text[:, D : D + 1]
    all_text = all_text[:, :D].astype(BF16)
    square = (64, 64)
    eye = lax.broadcasted_iota(jnp.int32, square, 0) == lax.broadcasted_iota(jnp.int32, square, 1)
    id_rows = jnp.dot(
        jnp.ones((8, 64), BF16), jnp.where(eye, id_column, 0.0).astype(BF16), preferred_element_type=F32
    )
    own_images = (lax.broadcasted_iota(jnp.int32, (8, 64), 0) + blk * 8).astype(F32)
    dots = lax.dot_general(image_unit.astype(BF16), all_text, NT, preferred_element_type=F32)
    image_weights = weights_of(dots, id_rows == own_images)
    image_grads = jnp.dot(image_weights, all_text, preferred_element_type=F32)
    image_out[...] = jnp.where(mp == 0, image_grads[:4], image_grads[4:])
    drain(before_units)
    for copy in unit_sends:
        copy.wait_recv()
    bands = units[...].astype(F32)
    all_units = jnp.concatenate([bands[:, :8], bands[:, 8:, :512]], axis=2).reshape(64, D).astype(BF16)
    dots = lax.dot_general(own_text[:, :D].astype(BF16), all_units, NT, preferred_element_type=F32)
    image_ids = lax.broadcasted_iota(jnp.int32, (8, 64), 1).astype(F32)
    text_weights = weights_of(dots, own_text[:, D : D + 1] == image_ids)
    text_out[...] = jnp.dot(text_weights, all_units, preferred_element_type=F32)[:4]

    drain(len(started))


CHANNELS = 160


def settle(*refs):
    copies = [pltpu.make_async_copy(refs[n], refs[3 + n], refs[6].at[n]) for n in range(3)]
    for copy in copies:
        copy.start()
    for copy in copies:
        copy.wait()


def per_device(x, tallies, slots, gain, w1, w2, texts, ids, mult, shift):
    vmem = pl.BlockSpec(memory_space=pltpu.VMEM)
    smem = pl.BlockSpec(memory_space=pltpu.SMEM)
    hbm = pl.BlockSpec(memory_space=pltpu.HBM)
    out = jax.ShapeDtypeStruct((4, D), F32)
    results = pl.pallas_call(
        kernel,
        out_shape=(out, out, out),
        in_specs=[hbm, smem, hbm, hbm, hbm, hbm, hbm, hbm, smem, smem],
        out_specs=(vmem, vmem, vmem),
        scratch_shapes=[
            pltpu.VMEM((ROWS, D), BF16),
            pltpu.VMEM((1, ROWS), jnp.int32),
            pltpu.VMEM((D,), F32),
            pltpu.VMEM((PIECE, 2152), BF16),
            pltpu.VMEM((PIECE, 2152), BF16),
            pltpu.VMEM((4, D), BF16),
            pltpu.VMEM((1, 4), jnp.int32),
            pltpu.VMEM((3, 4, 80, LANES), BF16),
            pltpu.VMEM((9, D, LANES), BF16),
            pltpu.VMEM((17, SET, LANES), BF16),
            pltpu.VMEM((D, D), BF16),
            pltpu.VMEM((2, ROWS, D), BF16),
            pltpu.VMEM((2, 8, ROWS), F32),
            pltpu.VMEM((2, 16, 640), BF16),
            pltpu.VMEM((8, 16, 640), BF16),
            pltpu.VMEM((8, 16, 640), BF16),
            pltpu.VMEM((2, 16, 256), BF16),
            pltpu.VMEM((2, 16, 384), BF16),
            pltpu.VMEM((8, 2, 16, 256), BF16),
            pltpu.VMEM((8, 2, 16, 384), BF16),
            pltpu.VMEM((64, 256), F32),
            pltpu.VMEM((16, 8, 256), F32),
            pltpu.SemaphoreType.DMA((7,)),
            pltpu.SemaphoreType.DMA((CHANNELS,)),
            pltpu.SemaphoreType.DMA((CHANNELS,)),
        ],
        compiler_params=pltpu.CompilerParams(
            collective_id=0, has_side_effects=True, vmem_limit_bytes=62 << 20
        ),
        name="siglip_step",
    )(
        x[0, 0],
        tallies[0],
        slots[0],
        gain,
        w1,
        w2.T,
        texts[0],
        ids,
        mult,
        shift,
    )
    results = pl.pallas_call(
        settle,
        out_shape=(out, out, out),
        in_specs=[hbm] * 3,
        out_specs=(hbm,) * 3,
        scratch_shapes=[pltpu.SemaphoreType.DMA((3,))],
        compiler_params=pltpu.CompilerParams(vmem_limit_bytes=62 << 20),
        name="settle",
    )(*results)
    return tuple(r[None] for r in results)


def solution(mesh):
    in_specs = (
        P("dp", "blk", None, None),
        P("dp", "blk"),
        P("dp", "blk", None),
        P(),
        P("dp", "mp"),
        P("mp", "dp"),
        P("dp", ("blk", "mp"), None),
        P("dp", ("blk", "mp")),
        P(),
        P(),
    )
    out_specs = (P("dp", ("blk", "mp"), None),) * 3
    return jax.shard_map(per_device, mesh=mesh, in_specs=in_specs, out_specs=out_specs, check_vma=False)
```

```python
import jax
import jax.numpy as jnp
from jax import lax
from jax.experimental import pallas as pl
from jax.experimental.pallas import tpu as pltpu
from jax.sharding import PartitionSpec as P

MESH = pl.DeviceIdType.MESH
F32 = jnp.float32
BF16 = jnp.bfloat16
D = 1152
ROWS = 640
PIECE = 36
SET = 4 * PIECE
LANES = 128
SIDES = (1, -1)
PASSED = ((0, 1), (1, 1), (-1, -1), (2, -1))
NT = (((1,), (1,)), ((), ()))


def column_origin(shape):
    r = lax.broadcasted_iota(jnp.int32, shape, 1)
    group = (r * 29128) >> 22
    inside = r - group * SET
    k = (inside * 1821) >> 16
    return r + ((group & 1) * 16 + 4 * k + (group >> 1) - group * 4 - k) * PIECE


def gelu(u):
    return 0.5 * u * (1.0 + jnp.tanh(0.7978845608028654 * (u + 0.044715 * (u * u * u))))


def two_bands(values):
    return jnp.concatenate([values[:, :640], values[:, 640:]], axis=0).astype(BF16)


def kernel(
    x_hbm,
    count_ref,
    slot_hbm,
    gain_hbm,
    w1_hbm,
    w2_hbm,
    text_hbm,
    ids_hbm,
    mult_ref,
    shift_ref,
    features_out,
    image_out,
    text_out,
    x_ref,
    slot_ref,
    gain_ref,
    w1_ref,
    w2_ref,
    text_ref,
    ids_ref,
    pieces,
    w1,
    w2,
    perm,
    normed,
    member,
    half_texts,
    texts,
    units,
    pooled_low,
    pooled_high,
    window_low,
    window_high,
    partial,
    returned,
    load_sem,
    send_sem,
    recv_sem,
):
    loads = [
        pltpu.make_async_copy(src, dst, load_sem.at[n])
        for n, (src, dst) in enumerate(
            [
                (w1_hbm, w1_ref),
                (w2_hbm, w2_ref),
                (text_hbm, text_ref),
                (ids_hbm, ids_ref),
                (slot_hbm, slot_ref),
                (gain_hbm, gain_ref),
                (x_hbm, x_ref),
            ]
        )
    ]
    for load in loads[:6]:
        load.start()
    blk, dp, mp = lax.axis_index("blk"), lax.axis_index("dp"), lax.axis_index("mp")
    y, c = lax.div(blk, 2), lax.rem(blk, 2)
    xl, z = lax.div(dp, 16), lax.rem(dp, 16)
    rho, k0 = lax.rem(z, 4), lax.div(z, 4)

    def dev(dy=0, dz=0, yy=None, cc=None, xx=None, mm=None):
        yy = lax.rem(y + dy + 8, 4) if yy is None else yy
        zz = lax.rem(z + dz + 32, 16)
        cc = c if cc is None else cc
        xx = xl if xx is None else xx
        mm = mp if mm is None else mm
        return {"blk": yy * 2 + cc, "dp": xx * 16 + zz, "mp": mm}

    def u_dev(off):
        return dev(dy=off * c, dz=off * (1 - c))

    def v_dev(off):
        return dev(dy=off * (1 - c), dz=off * c)

    started = []
    channels = [0]

    def send(src, dst, where, when=None):
        ch = channels[0]
        channels[0] += 1
        copy = pltpu.make_async_remote_copy(
            src_ref=src,
            dst_ref=dst,
            send_sem=send_sem.at[ch],
            recv_sem=recv_sem.at[ch],
            device_id=where,
            device_id_type=MESH,
        )
        if when is None:
            copy.start()
        else:
            pl.when(when)(copy.start)
        started.append((copy, when))
        return copy

    drained = [0]

    def drain(end):
        for copy, when in started[drained[0] : end]:
            if when is None:
                copy.wait_send()
            else:
                pl.when(when)(copy.wait_send)
        drained[0] = end

    barrier = pltpu.get_barrier_semaphore()
    peers = [dev(dz=4), dev(dz=12)]
    for dx in (0, 1):
        for dz in (-2, -1, 0, 1, 2):
            for dc, dm in ((0, 0), (0, 1), (1, 0)):
                if (dx, dz, dc, dm) != (0, 0, 0, 0):
                    xx, cc, mm = lax.rem(xl + dx, 2), lax.rem(c + dc, 2), lax.rem(mp + dm, 2)
                    peers.append(dev(dz=dz, xx=xx, cc=cc, mm=mm))
    for dy in (1, 2, 3):
        for dc in (0, 1):
            peers.append(dev(dy=dy, cc=lax.rem(c + dc, 2)))
    for peer in peers:
        pl.semaphore_signal(barrier, inc=1, device_id=peer, device_id_type=MESH)

    def two_tiles(a, b):
        both = [a.astype(F32), b.astype(F32), jnp.zeros((8, LANES), F32)]
        return jnp.concatenate(both, axis=0).astype(BF16)

    def tile_of(ref, index):
        return ref[:, pl.ds(pl.multiple_of(index * LANES, LANES), LANES)]

    def odd_tile(ref):
        part = ref[:, 2048:2152].astype(F32)
        return jnp.concatenate([part, jnp.zeros((PIECE, 24), F32)], axis=1)

    is_even = c == 0
    core = dev(cc=1 - c)
    partner = dev(xx=1 - xl)

    def push(ref, where, when=None):
        return send(ref, ref, where, when)

    def first_phase(j, when=None):
        return [push(pieces.at[j, k0], dev(dz=dz), when) for dz in (4, 12)]

    def first_onward(j, copies, when=None):
        for copy in copies:
            if when is None:
                copy.wait_recv()
            else:
                pl.when(when)(copy.wait_recv)
        return [
            push(pieces.at[j, lax.rem(k0 + 3, 4), pl.ds(0, 48)], dev(dz=4), when),
            push(pieces.at[j, lax.rem(k0 + 1, 4), pl.ds(48, 32)], dev(dz=12), when),
        ]

    chunk = 128

    def perm_step(i, _):
        rows = pl.ds(pl.multiple_of(i * chunk, chunk), chunk)
        origin = lax.broadcasted_iota(jnp.int32, (chunk, D), 0) + i * chunk
        perm[rows, :] = jnp.where(origin == column_origin((chunk, D)), 1.0, 0.0).astype(BF16)
        return 0

    loads[0].wait()
    loads[6].start()
    pieces[0, k0] = two_tiles(tile_of(w1_ref, c * 8 + y), tile_of(w1_ref, c * 8 + 4 + y))
    pl.semaphore_wait(barrier, len(peers))
    first0 = first_phase(0)
    loads[1].wait()
    pieces[1, k0] = two_tiles(odd_tile(w1_ref), odd_tile(w2_ref))
    pieces[2, k0] = two_tiles(tile_of(w2_ref, c * 8 + y), tile_of(w2_ref, c * 8 + 4 + y))
    first1 = first_phase(1, is_even)
    first2 = first_phase(2)
    lax.fori_loop(0, D // chunk, perm_step, 0)
    for load in loads[2:]:
        load.wait()
    gain = gain_ref[...].reshape(1, D)
    band = ROWS // 2

    def normalise(i):
        rows = pl.ds(i * band, band)
        values = x_ref[rows, :].astype(F32)
        center = values - jnp.mean(values, axis=1, keepdims=True)
        spread = jnp.mean(center * center, axis=1, keepdims=True)
        scaled = (center * lax.rsqrt(spread + 1e-06) * gain).astype(BF16)
        normed[c, rows, :] = jnp.dot(scaled, perm[...], preferred_element_type=F32).astype(BF16)

    normalise(0)
    onward0 = first_onward(0, first0)
    onward1 = first_onward(1, first1, is_even)
    onward2 = first_onward(2, first2)
    normalise(1)
    normed_send = push(normed.at[c], core)

    def rows_of(r, x=None):
        if x is None:
            return pl.ds(pl.multiple_of(r * 2 * SET, 16), 2 * SET)
        return pl.ds(pl.multiple_of((r * 2 + x) * SET, 16), SET)

    def place(a, o=0):
        yy = lax.rem(y + 8 - a * c - o * (1 - c), 4)
        rr = lax.rem(rho + 8 - a * (1 - c) - o * c, 4)
        return yy, rr

    def block(group, where, x=None):
        yy, rr = where
        return w1.at[group * 4 + yy, rows_of(rr, x)]

    def stacked(j, t):
        parts = [pieces[j, k].astype(F32)[PIECE * t : PIECE * (t + 1)] for k in range(4)]
        return jnp.concatenate(parts, axis=0).astype(BF16)

    along = {}

    def both_ways(group, a):
        ref = block(group, place(a))
        along[group, a, 1] = push(ref, v_dev(1))
        along[group, a, -1] = push(ref, v_dev(-1))

    for copy in onward0:
        copy.wait_recv()
    for t in range(2):
        w1[t * 4 + y, rows_of(rho, xl), :] = stacked(0, t)
    a1 = push(block(0, place(0), xl), partner)
    own1 = block(1, place(0), xl)
    across = {0: push(own1, partner)}
    b1 = {o: push(own1, u_dev(o)) for o in (1, -1, -2)}

    text = text_ref[...].astype(F32)
    text = text * lax.rsqrt(jnp.sum(text * text, axis=1, keepdims=True) + 1e-06)
    diagonal = lax.broadcasted_iota(jnp.int32, (4, 4), 0) == lax.broadcasted_iota(jnp.int32, (4, 4), 1)
    ids = jnp.sum(jnp.where(diagonal, jnp.broadcast_to(ids_ref[...], (4, 4)), 0).astype(F32), axis=1, keepdims=True)
    text_rows = jnp.concatenate([text, jnp.broadcast_to(ids, (4, LANES))], axis=1)
    blank = jnp.zeros((4, D + LANES), F32)
    own_text = jnp.concatenate([text_rows, blank], axis=0)
    placed_text = jnp.where(mp == 0, own_text, jnp.concatenate([blank, text_rows], axis=0))
    half_texts[mp] = two_bands(placed_text)
    half_send = push(half_texts.at[mp], dev(mm=1 - mp))
    positions = lax.broadcasted_iota(jnp.int32, (8, ROWS), 1)
    slots = lax.broadcasted_iota(jnp.int32, (8, ROWS), 0)
    is_member = (jnp.broadcast_to(slot_ref[...], (8, ROWS)) == slots) & (positions < count_ref[0])
    own_member = jnp.where(is_member, 1.0, 0.0).astype(F32)
    member[c] = own_member
    member_send = push(member.at[c], core)
    own_sizes = jnp.maximum(jnp.sum(own_member, axis=1, keepdims=True), 1.0)

    def onward_pair(ref_at, copies, where, when=None):
        out = []
        for o in SIDES:
            if when is None:
                copies[o].wait_recv()
            else:
                pl.when(when)(copies[o].wait_recv)
            out.append(push(ref_at(o, 0 if o == 1 else 1), where(o), when))
        return out

    def onward_pair(ref_at, copies, where, when=None):
        out = []
        for o in SIDES:
            if when is None:
                copies[o].wait_recv()
            else:
                pl.when(when)(copies[o].wait_recv)
            out.append(push(ref_at(o, 0 if o == 1 else 1), where(o), when))
        return out

    def pass_on(group, a, o):
        along[group, a, o].wait_recv()
        along[group, a, 2 * o] = push(block(group, place(a, o)), v_dev(o))

    last = []

    def finish(a, o):
        last.append(push(block(1, place(a, o), xl), partner))

    def onward_pair(ref_at, copies, where, when=None):
        out = []
        for o in SIDES:
            if when is None:
                copies[o].wait_recv()
            else:
                pl.when(when)(copies[o].wait_recv)
            out.append(push(ref_at(o, 0 if o == 1 else 1), where(o), when))
        return out

    def pass_on(group, a, o):
        along[group, a, o].wait_recv()
        along[group, a, 2 * o] = push(block(group, place(a, o)), v_dev(o))

    last = []

    def finish(a, o):
        last.append(push(block(1, place(a, o), xl), partner))

    a1.wait_recv()
    pair = block(0, place(0))
    a2 = {o: push(pair, u_dev(o)) for o in (1, -1, 2)}
    both_ways(0, 0)
    across[0].wait_recv()
    both_ways(1, 0)
    for o in SIDES:
        b1[o].wait_recv()
        single = block(1, place(o), xl)
        along[1, o, 1] = push(single, v_dev(1))
        along[1, o, -1] = push(single, v_dev(-1))
        finish(o, 0)
    b1[-2].wait_recv()
    across[2] = push(block(1, place(2), xl), partner)
    for a in (1, -1, 2):
        a2[a].wait_recv()
        both_ways(0, a)
    for copy in onward1:
        pl.when(is_even)(copy.wait_recv)

    @pl.when(is_even)
    def _():
        w1[8, rows_of(rho, xl), :] = stacked(1, 0)
        w2[16] = stacked(1, 1)

    @pl.when(c == 1)
    def _():
        w1[8] = jnp.zeros((D, LANES), BF16)

    odd1 = push(w1.at[8, rows_of(rho, xl)], partner, is_even)
    pass_on(0, *PASSED[0])
    pass_on(1, *PASSED[0])
    for a in SIDES:
        for o in SIDES:
            along[1, a, o].wait_recv()
            if a == o:
                along[1, a, 2 * o] = push(block(1, place(a, o), xl), v_dev(o))
            finish(a, o)
    pl.when(is_even)(odd1.wait_recv)
    odd2 = {o: push(w1.at[8, rows_of(rho)], dev(dz=o), is_even) for o in SIDES}
    across[2].wait_recv()
    both_ways(1, 2)
    for a, o in PASSED[1:]:
        pass_on(0, a, o)
    for copy in onward2:
        copy.wait_recv()
    for t in range(2):
        w2[c * 8 + y * 2 + t] = stacked(2, t)
    own2 = w2.at[pl.ds(c * 8 + y * 2, 2)]
    w2_sides = {o: push(own2, dev(dy=o)) for o in SIDES}
    odd3 = onward_pair(lambda o, x: w1.at[8, rows_of(lax.rem(rho + 4 - o, 4), x)], odd2, lambda o: dev(dz=o), is_even)
    pass_on(1, *PASSED[3])
    for a in SIDES:
        along[1, a, 2 * a].wait_recv()
        finish(a, 2 * a)

    member_send.wait_recv()
    normed_send.wait_recv()
    nothing = jnp.zeros((8, ROWS), F32)
    members = [
        jnp.concatenate([member[0], nothing], axis=0).astype(BF16),
        jnp.concatenate([nothing, member[1]], axis=0).astype(BF16),
    ]
    sizes = [jnp.maximum(jnp.sum(member[q], axis=1, keepdims=True), 1.0) for q in range(2)]

    def tile_work(tiles):
        weights = jnp.concatenate([w1[t] for t in tiles], axis=1)
        sums = jnp.zeros((16, LANES * len(tiles)), F32)
        for q in range(2):
            hidden = gelu(jnp.dot(normed[q], weights, preferred_element_type=F32)).astype(BF16)
            sums = sums + jnp.dot(members[q], hidden, preferred_element_type=F32)
        return sums / jnp.concatenate(sizes, axis=0)

    own_window = xl * 4

    def reach(n, cc):
        return (0, 1, -1)[n] if n < 3 else 2 - 4 * cc

    def window_phase(sums, bands, pool, there):
        for q in range(2):
            own = sums[8 * q : 8 * q + 8]
            pool[q] = jnp.concatenate([own[:, :bands], own[:, bands:]], axis=0).astype(BF16)
        there[own_window, c] = pool[c]
        out = []
        for n in (3, 1, 2, 0):
            for dx in (0, 1):
                for dc in (0, 1):
                    if (n, dx, dc) == (0, 0, 0):
                        continue
                    cc = lax.rem(c + dc, 2)
                    where = dev(dz=reach(n, cc), xx=lax.rem(xl + dx, 2), cc=cc)
                    out.append(send(pool.at[cc], there.at[own_window + n, c], where))
        return out

    for key, copy in along.items():
        if key[0] == 0 and key[1:] not in PASSED:
            copy.wait_recv()
    low_sums = tile_work((0, 1, 2, 3))
    low_sends = window_phase(low_sums, 256, pooled_low, window_low)
    w2_far = onward_pair(lambda o, x: w2.at[c * 8 + lax.rem(y + 4 - o, 4) * 2 + x], w2_sides, lambda o: dev(dy=o))
    half_send.wait_recv()
    texts[blk] = half_texts[0] + half_texts[1]
    text_sides = {o: push(texts.at[blk], dev(dy=o)) for o in SIDES}
    text_sends = [push(texts.at[blk], core)]
    for copy in last:
        copy.wait_recv()
    for key, copy in along.items():
        if key[0] == 1 and key[1:] not in PASSED and (key[1] in (0, 2)):
            copy.wait_recv()
    for copy in odd3:
        pl.when(is_even)(copy.wait_recv)
    high_sums = tile_work((4, 5, 6, 7, 8))
    high_sums = jnp.concatenate([high_sums, jnp.zeros((16, LANES), F32)], axis=1)
    before_window = len(started)
    high_sends = window_phase(high_sums, 384, pooled_high, window_high)
    patch_mean = jnp.dot(own_member.astype(BF16), x_ref[...], preferred_element_type=F32) / own_sizes
    for o in SIDES:
        text_sides[o].wait_recv()
    turn = 1 - 2 * c
    text_far = push(texts.at[lax.rem(y + 4 - turn, 4) * 2 + c], dev(dy=turn))

    def text_of(dy):
        return texts.at[lax.rem(y + dy + 4, 4) * 2 + c]

    text_sends += [push(text_of(o), core) for o in SIDES]
    for copy in w2_far:
        copy.wait_recv()
    w2_core = push(w2.at[pl.ds(c * 8, 8)], core)
    w2_odd = push(w2.at[16], core, is_even)
    w2_core.wait_recv()
    pl.when(c == 1)(w2_odd.wait_recv)
    bands = []
    for tiles in ((0, 1, 4, 5, 6), (2, 3, 7, 8, 9)):
        parts = []
        for half in range(2):
            for n in tiles:
                if n < 8:
                    parts.append(w2[half * 8 + (n % 4) * 2 + n // 4])
                elif n == 8 and half == 0:
                    parts.append(w2[16])
                else:
                    parts.append(jnp.zeros((SET, LANES), BF16))
        bands.append(jnp.concatenate(parts, axis=1))
    drain(before_window)
    for copy in low_sends + high_sends:
        copy.wait_recv()
    parts = []
    for half in range(2):
        parts += [window_low[:, half].reshape(128, 256), window_high[:, half].reshape(128, 384)]
    gathered = jnp.concatenate(parts, axis=1)
    over = [lax.dot_general(gathered, band, NT, preferred_element_type=F32).reshape(8, 16, SET) for band in bands]
    result = (over[0][:, :8] + over[1][:, 8:]).reshape(64, SET)
    partial[...] = jnp.concatenate([result, jnp.zeros((64, 256 - SET), F32)], axis=1)
    before_returned = len(started)
    my_set = mp * 8 + rho * 2 + xl
    returned_sends = []
    for n in (3, 1, 2, 0):
        for dx in (0, 1):
            xx = lax.rem(xl + dx, 2)
            rows = partial.at[pl.ds(pl.multiple_of((xx * 4 + n) * 8, 8), 8)]
            for dm in (0, 1):
                if (n, dx, dm) == (0, 0, 0):
                    continue
                where = dev(dz=-reach(n, c), xx=xx, mm=lax.rem(mp + dm, 2))
                returned_sends.append(send(rows, returned.at[my_set], where))
    returned[my_set] = partial[pl.ds(pl.multiple_of(xl * 32, 8), 8), :]
    text_far.wait_recv()
    text_sends.append(push(text_of(2), core))
    drain(before_returned)
    for copy in returned_sends:
        copy.wait_recv()
    sums = [returned[n] + returned[8 + n] for n in range(8)]
    columns = []
    for x in range(2):
        for zz in range(16):
            k, r = zz // 4, zz % 4
            columns.append(sums[r * 2 + x][:, PIECE * k : PIECE * (k + 1)])
    features = jnp.concatenate(columns, axis=1) + patch_mean
    features_out[...] = jnp.where(mp == 0, features[:4], features[4:])

    image_unit = features * lax.rsqrt(jnp.sum(features * features, axis=1, keepdims=True) + 1e-06)
    units[blk] = two_bands(jnp.concatenate([image_unit, jnp.zeros((8, LANES), F32)], axis=1))
    before_units = len(started)
    unit_sends = []
    for dy in (2, 1, 3, 0):
        for dc in (1, 0):
            if (dy, dc) != (0, 0):
                where = dev(dy=dy, cc=lax.rem(c + dc, 2))
                unit_sends.append(send(units.at[blk], units.at[blk], where))
    for copy in text_sends:
        copy.wait_recv()
    mult, shift = mult_ref[0], shift_ref[0]

    def weights_of(dots, same):
        signs = jnp.where(same, 1.0, -1.0).astype(F32)
        logits = mult * dots + shift
        return (mult * -signs * jax.nn.sigmoid(-signs * logits)).astype(BF16)

    captions = texts[...].astype(F32)
    all_text = jnp.concatenate([captions[:, :8], captions[:, 8:]], axis=2).reshape(64, D + LANES)
    id_column = all_text[:, D : D + 1]
    all_text = all_text[:, :D].astype(BF16)
    square = (64, 64)
    eye = lax.broadcasted_iota(jnp.int32, square, 0) == lax.broadcasted_iota(jnp.int32, square, 1)
    id_rows = jnp.dot(
        jnp.ones((8, 64), BF16), jnp.where(eye, id_column, 0.0).astype(BF16), preferred_element_type=F32
    )
    own_images = (lax.broadcasted_iota(jnp.int32, (8, 64), 0) + blk * 8).astype(F32)
    dots = lax.dot_general(image_unit.astype(BF16), all_text, NT, preferred_element_type=F32)
    image_weights = weights_of(dots, id_rows == own_images)
    image_grads = jnp.dot(image_weights, all_text, preferred_element_type=F32)
    image_out[...] = jnp.where(mp == 0, image_grads[:4], image_grads[4:])
    drain(before_units)
    for copy in unit_sends:
        copy.wait_recv()
    bands = units[...].astype(F32)
    all_units = jnp.concatenate([bands[:, :8], bands[:, 8:, :512]], axis=2).reshape(64, D).astype(BF16)
    dots = lax.dot_general(own_text[:, :D].astype(BF16), all_units, NT, preferred_element_type=F32)
    image_ids = lax.broadcasted_iota(jnp.int32, (8, 64), 1).astype(F32)
    text_weights = weights_of(dots, own_text[:, D : D + 1] == image_ids)
    text_out[...] = jnp.dot(text_weights, all_units, preferred_element_type=F32)[:4]

    drain(len(started))


CHANNELS = 160


def settle(*refs):
    for n in range(3):
        refs[3 + n][...] = refs[n][...]


def per_device(x, tallies, slots, gain, w1, w2, texts, ids, mult, shift):
    vmem = pl.BlockSpec(memory_space=pltpu.VMEM)
    smem = pl.BlockSpec(memory_space=pltpu.SMEM)
    hbm = pl.BlockSpec(memory_space=pltpu.HBM)
    out = jax.ShapeDtypeStruct((4, D), F32)
    results = pl.pallas_call(
        kernel,
        out_shape=(out, out, out),
        in_specs=[hbm, smem, hbm, hbm, hbm, hbm, hbm, hbm, smem, smem],
        out_specs=(vmem, vmem, vmem),
        scratch_shapes=[
            pltpu.VMEM((ROWS, D), BF16),
            pltpu.VMEM((1, ROWS), jnp.int32),
            pltpu.VMEM((D,), F32),
            pltpu.VMEM((PIECE, 2152), BF16),
            pltpu.VMEM((PIECE, 2152), BF16),
            pltpu.VMEM((4, D), BF16),
            pltpu.VMEM((1, 4), jnp.int32),
            pltpu.VMEM((3, 4, 80, LANES), BF16),
            pltpu.VMEM((9, D, LANES), BF16),
            pltpu.VMEM((17, SET, LANES), BF16),
            pltpu.VMEM((D, D), BF16),
            pltpu.VMEM((2, ROWS, D), BF16),
            pltpu.VMEM((2, 8, ROWS), F32),
            pltpu.VMEM((2, 16, 640), BF16),
            pltpu.VMEM((8, 16, 640), BF16),
            pltpu.VMEM((8, 16, 640), BF16),
            pltpu.VMEM((2, 16, 256), BF16),
            pltpu.VMEM((2, 16, 384), BF16),
            pltpu.VMEM((8, 2, 16, 256), BF16),
            pltpu.VMEM((8, 2, 16, 384), BF16),
            pltpu.VMEM((64, 256), F32),
            pltpu.VMEM((16, 8, 256), F32),
            pltpu.SemaphoreType.DMA((7,)),
            pltpu.SemaphoreType.DMA((CHANNELS,)),
            pltpu.SemaphoreType.DMA((CHANNELS,)),
        ],
        compiler_params=pltpu.CompilerParams(
            collective_id=0, has_side_effects=True, vmem_limit_bytes=62 << 20
        ),
        name="siglip_step",
    )(
        x[0, 0],
        tallies[0],
        slots[0],
        gain,
        w1,
        w2.T,
        texts[0],
        ids,
        mult,
        shift,
    )
    results = pl.pallas_call(
        settle,
        out_shape=(out, out, out),
        in_specs=[vmem] * 3,
        out_specs=(vmem,) * 3,
        compiler_params=pltpu.CompilerParams(vmem_limit_bytes=62 << 20),
        name="settle",
    )(*results)
    return tuple(r[None] for r in results)


def solution(mesh):
    in_specs = (
        P("dp", "blk", None, None),
        P("dp", "blk"),
        P("dp", "blk", None),
        P(),
        P("dp", "mp"),
        P("mp", "dp"),
        P("dp", ("blk", "mp"), None),
        P("dp", ("blk", "mp")),
        P(),
        P(),
    )
    out_specs = (P("dp", ("blk", "mp"), None),) * 3
    return jax.shard_map(per_device, mesh=mesh, in_specs=in_specs, out_specs=out_specs, check_vma=False)
```
